32 devices in a mesh: snap: 8 (over z, x), mesh: 4 (over y, core).
Axes of the slice: x: 2, y: 2, z: 4, core: 2. Of those that a mesh axis runs over, the one named last changes fastest.
Arguments:
- snapshots: float32 [12288, 1024], P('mesh', 'snap'), may hold values from -6 to 6
- region_ids: int32 [24, 512], P('mesh'), may hold values from 0 to 7
- conductivity: float32 [8], replicated, may hold values from 0.2 to 5
Outputs:
- gram: float32 [1024, 1024], P('snap', 'mesh')
The draws below stay inside these ranges and needn't reach their ends.
All inputs are finite; a program needn't handle non-finite values.
Results may differ from the reference program's by a relative error of at most 0.0003.
Values sent between devices are 32-bit elements; how exact they have to be, the bound alone decides.
No kernel may reach another device: no remote copies, remote signals or barrier semaphores. Data moves between devices by JAX's collectives and lax.ppermute only.
A program may use at most 128 MiB of HBM per device.

```python
import math
import jax
import jax.numpy as jnp
from jax import lax

RY = 512
SNAP_DEV = 128
REGIONS = 8
NX = 24
NODES = 12288
SNAPS = 1024


def set_ends(entries, stream_key, low, top_value):
    longest = entries.shape.index(max(entries.shape))
    spots = []
    for shift in (0, 1):
        where = [jax.random.randint(jax.random.fold_in(stream_key, axis), (), 0, length) for axis, length in enumerate(entries.shape)]
        where[longest] = (where[longest] + shift) % entries.shape[longest]
        spots.append(tuple(where))
    return entries.at[spots[0]].set(low).at[spots[1]].set(top_value)


def block_scale(stream_key, dims, cuts, smallest, largest):
    def one(position, parts):
        steps = jax.random.uniform(jax.random.fold_in(jax.random.fold_in(stream_key, 6), position), (parts,), jnp.float32, smallest / len(cuts), largest / len(cuts))
        return jnp.repeat(jnp.exp(steps), dims[position] // parts).reshape((-1,) + (1,) * (len(dims) - position - 1))

    gain = one(*cuts[0])
    for cut in cuts[1:]:
        gain = gain * one(*cut)
    return gain


def normal_values(rng, dims, spread, reach, cuts=(), kind=jnp.bfloat16):
    factor_of = block_scale(rng, dims, cuts, -0.22, 0.18) if cuts else 1.0
    values = jax.random.normal(rng, dims, jnp.float32) * spread * factor_of
    return jnp.minimum(jnp.maximum(values, -reach), reach).astype(kind)


def setup_inputs(seed: int = 0) -> dict:
    key_of = jax.random.split(jax.random.key(seed), 4)
    snapshots = normal_values(key_of[0], (NODES, SNAPS), 1.0, 6.0, ((0, 4), (1, 8)), jnp.float32)
    region_ids = set_ends(jax.random.randint(key_of[1], (NX, RY), 0, REGIONS), jax.random.fold_in(key_of[1], 1), 0, REGIONS - 1).astype(jnp.int32)
    conductivity = jnp.clip(jnp.exp(jax.random.uniform(key_of[2], (REGIONS,), jnp.float32, math.log(0.2), math.log(5.0))), 0.2, 5.0)
    return {"snapshots": snapshots, "region_ids": region_ids, "conductivity": conductivity}


def weights_of(region_ids, conductivity):
    table = jnp.arange(conductivity.shape[0], dtype=jnp.int32)
    picked = jnp.where(region_ids[:, :, None] == table[None, None, :], conductivity[None, None, :], jnp.zeros((), conductivity.dtype))
    return lax.optimization_barrier(jnp.sum(picked, axis=-1)) / 36.0

def element_terms(field, below, weight):
    lower = jnp.concatenate([field, below[None]], 0)
    padded = jnp.pad(lower, ((0, 0), (0, 1), (0, 0)))
    corner_a = padded[:-1, :-1]
    corner_b = padded[:-1, 1:]
    corner_e = padded[1:, :-1]
    corner_d = padded[1:, 1:]
    scaled = weight[:, :, None]
    to_a = scaled * (4.0 * corner_a + 2.0 * corner_b + 2.0 * corner_e + corner_d)
    to_b = scaled * (2.0 * corner_a + 4.0 * corner_b + corner_e + 2.0 * corner_d)
    to_e = scaled * (2.0 * corner_a + corner_b + 4.0 * corner_e + 2.0 * corner_d)
    to_d = scaled * (corner_a + 2.0 * corner_b + 2.0 * corner_e + 4.0 * corner_d)
    total = jnp.pad(to_a, ((0, 1), (0, 1), (0, 0))) + jnp.pad(to_b, ((0, 1), (1, 0), (0, 0)))
    total = total + jnp.pad(to_e, ((1, 0), (0, 1), (0, 0))) + jnp.pad(to_d, ((1, 0), (1, 0), (0, 0)))
    return total

def reference(snapshots, region_ids, conductivity):
    weight = weights_of(region_ids, conductivity)
    blocks = SNAPS // SNAP_DEV

    def one_block(index):
        start = (index * SNAP_DEV).astype(jnp.int32)
        columns = lax.dynamic_slice_in_dim(snapshots, start, SNAP_DEV, 1)
        field = columns.reshape(NX, RY, SNAP_DEV)
        below = jnp.zeros((RY, SNAP_DEV), snapshots.dtype)
        total = element_terms(field, below, weight)
        return total[:NX, :RY].reshape(NODES, SNAP_DEV)
    stacked = lax.map(one_block, jnp.arange(blocks, dtype=jnp.int32))
    panel = jnp.transpose(stacked, (1, 0, 2)).reshape(NODES, SNAPS)
    gram = jnp.dot(snapshots.T, panel, precision=lax.Precision.HIGHEST, preferred_element_type=jnp.float32)
    return gram / math.sqrt(NODES)
```

```python
import math

import jax
import jax.numpy as jnp
from jax import lax
from jax.experimental import pallas as pl
from jax.experimental.pallas import tpu as pltpu
from jax.sharding import Mesh
from jax.sharding import PartitionSpec as P


def passed_along(value, axis, steps):
    count = lax.axis_size(axis)
    first, last = (max(0, -steps), min(count, count - steps))
    return lax.ppermute(value, axis, [(source, source + steps) for source in range(first, last)])


def from_behind(block, axis, distance):
    devices = range(lax.axis_size(axis))
    route = [((i - distance) % len(devices), i) for i in devices]
    return lax.ppermute(block, axis, route)


def weights_of(region_ids, conductivity):
    table = jnp.arange(conductivity.shape[0], dtype=jnp.int32)
    picked = jnp.where(
        region_ids[:, :, None] == table[None, None, :],
        conductivity[None, None, :],
        jnp.zeros((), conductivity.dtype),
    )
    return jnp.sum(picked, axis=-1) / 36.0


def element_terms(field, below, weight):
    lower = jnp.concatenate([field, below[None]], 0)
    padded = jnp.pad(lower, ((0, 0), (0, 1), (0, 0)))
    corner_a = padded[:-1, :-1]
    corner_b = padded[:-1, 1:]
    corner_e = padded[1:, :-1]
    corner_d = padded[1:, 1:]
    scaled = weight[:, :, None]
    to_a = scaled * (4.0 * corner_a + 2.0 * corner_b + 2.0 * corner_e + corner_d)
    to_b = scaled * (2.0 * corner_a + 4.0 * corner_b + corner_e + 2.0 * corner_d)
    to_e = scaled * (2.0 * corner_a + corner_b + 4.0 * corner_e + 2.0 * corner_d)
    to_d = scaled * (corner_a + 2.0 * corner_b + 2.0 * corner_e + 4.0 * corner_d)
    total = jnp.pad(to_a, ((0, 1), (0, 1), (0, 0))) + jnp.pad(to_b, ((0, 1), (1, 0), (0, 0)))
    total = (
        total + jnp.pad(to_e, ((1, 0), (0, 1), (0, 0))) + jnp.pad(to_d, ((1, 0), (1, 0), (0, 0)))
    )
    return total


def contract(left, right):
    return lax.dot_general(
        left,
        right,
        (((0,), (0,)), ((), ())),
        precision=lax.Precision.HIGHEST,
        preferred_element_type=jnp.float32,
    )


def local_ring(snapshots, region_ids, conductivity):
    strip, width = region_ids.shape
    node_rows, group_cols = snapshots.shape
    field = snapshots.reshape(strip, width, group_cols)
    weight = weights_of(region_ids, conductivity)
    below = passed_along(field[0], "mesh", -1)
    total = element_terms(field, below, weight)
    carried = passed_along(total[strip, :width], "mesh", 1)
    inner = total[:strip, :width]
    panel = jnp.concatenate([inner[:1] + carried[None], inner[1:]], 0).reshape(
        node_rows, group_cols
    )
    count = lax.axis_size("snap")
    group = lax.axis_index("snap")
    reach = count // 2

    def place(partial_value, moving, step):
        tile = contract(snapshots, moving)
        source = (group - step) % count * group_cols
        return lax.dynamic_update_slice(partial_value, tile, (jnp.int32(0), source))

    partial_value = place(jnp.zeros((group_cols, group_cols * count), jnp.float32), panel, 0)

    def turn(step, carry):
        moving, partial_value = carry
        moving = from_behind(moving, "snap", 1)
        return (moving, place(partial_value, moving, step))

    _, partial_value = lax.fori_loop(1, reach + 1, turn, (panel, partial_value))
    blocks = jnp.transpose(partial_value.reshape(group_cols, count, group_cols), (1, 2, 0))
    target = jnp.arange(count, dtype=jnp.int32)
    offset = (group - target) % count
    valid = (offset >= 1) & (offset <= count - 1 - reach)
    outgoing = jnp.where(valid[:, None, None], blocks, jnp.zeros((), jnp.float32))
    incoming = lax.all_to_all(outgoing, "snap", split_axis=0, concat_axis=0, tiled=True)
    partial_value = partial_value + jnp.transpose(incoming, (1, 0, 2)).reshape(
        group_cols, count * group_cols
    )
    summed = lax.psum_scatter(partial_value, "mesh", scatter_dimension=1, tiled=True)
    total_nodes = node_rows * lax.axis_size("mesh")
    return summed / math.sqrt(total_nodes)


ALL = ("h", "l", "x", "y", "c")
PLACE = ("l", "x")
TILE = ("y", "c")
GROUP = 128
STRIP = 128
SEAM = 16


def flat(h, l, x, y, c):
    return (((h * 2 + l) * 2 + x) * 2 + y) * 2 + c


def crossing(outer, flip):
    pairs = []
    for h in range(2):
        l = h if outer else 1 - h
        for x in range(2):
            for y in range(2):
                for c in range(2):
                    pairs.append((flat(h, l, x, y, c), flat(1 - h, h, x ^ flip, y, c)))
    return pairs


def split(value):
    high = value.astype(jnp.bfloat16)
    return high, (value - high.astype(jnp.float32)).astype(jnp.bfloat16)


def product(left_high, left_low, right_high, right_low):
    def one(a, b):
        return lax.dot_general(
            a, b, (((0,), (0,)), ((), ())), preferred_element_type=jnp.float32
        )

    return one(left_high, right_high) + one(left_high, right_low) + one(left_low, right_high)


def own_kernel(
    rows, seam_ref, field_ref, above_ref, below_ref, weight_ref, high_ref, low_ref, gram_ref, sh, sl
):
    wide = STRIP + 16
    line_number = lax.broadcasted_iota(jnp.int32, (SEAM, GROUP), 0)

    def line(main, left, right):
        return jnp.concatenate(
            [
                jnp.broadcast_to(left, (8, GROUP)),
                main,
                jnp.broadcast_to(right, (8, GROUP)),
            ],
            0,
        )

    def halo(ref, g):
        return line(ref[g, :STRIP], ref[g, STRIP : STRIP + 1], ref[g, STRIP + 1 : STRIP + 2])

    body = rows * STRIP
    for g in range(4):
        columns = slice(g * GROUP, (g + 1) * GROUP)
        before = halo(above_ref, g)
        before_up = pltpu.roll(before, wide - 1, 0)
        carried = carried_next = None
        seam = jnp.zeros((SEAM, GROUP), jnp.float32)
        for r in range(-1, rows):
            if r + 1 < rows:
                main = field_ref[g, (r + 1) * STRIP : (r + 2) * STRIP]
                after = line(
                    main,
                    field_ref[g, body + r + 1 : body + r + 2],
                    field_ref[g, body + 8 + r + 1 : body + 8 + r + 2],
                )
                high, low = split(main)
                sh[(r + 1) * STRIP : (r + 2) * STRIP, columns] = high
                sl[(r + 1) * STRIP : (r + 2) * STRIP, columns] = low
            else:
                after = halo(below_ref, g)
            after_up = pltpu.roll(after, wide - 1, 0)
            weight = weight_ref[r + 1]
            top, top_up = 2.0 * before + after, 2.0 * before_up + after_up
            to_a, to_b = weight * (2.0 * top + top_up), weight * (top + 2.0 * top_up)
            if r >= 0:
                from_left = pltpu.roll(to_b + carried_next, 1, 0)
                total = to_a + carried + from_left
                beside = (
                    seam_ref[0] * from_left[8 + STRIP : 9 + STRIP] + seam_ref[1] * from_left[8:9]
                )
                seam = jnp.where(line_number == r, beside, seam)
                high, low = split(total[8 : 8 + STRIP])
                high_ref[r * STRIP : (r + 1) * STRIP, columns] = high
                low_ref[r * STRIP : (r + 1) * STRIP, columns] = low
            low_end, low_up = before + 2.0 * after, before_up + 2.0 * after_up
            carried = weight * (2.0 * low_end + low_up)
            carried_next = weight * (low_end + 2.0 * low_up)
            before, before_up = after, after_up
        high, low = split(seam)
        high_ref[body : body + SEAM, columns] = high
        low_ref[body : body + SEAM, columns] = low
    for a in range(2):
        left = slice(a * 256, (a + 1) * 256)
        for b in range(2):
            right = slice(b * 256, (b + 1) * 256)
            tile = product(
                sh[:, left], sl[:, left], high_ref[:body, right], low_ref[:body, right]
            )
            for i in range(2):
                for j in range(2):
                    gram_ref[(2 * a + i) * 4 + 2 * b + j] = tile[
                        i * GROUP : (i + 1) * GROUP, j * GROUP : (j + 1) * GROUP
                    ]


def cross_kernel(place_ref, high_ref, low_ref, s0, s1, s2, s3, gram_ref):
    for pair, (first, second) in enumerate(((s0, s1), (s2, s3))):
        h0, l0 = split(first[...])
        h1, l1 = split(second[...])
        sh = jnp.concatenate([h0, h1], 1)
        sl = jnp.concatenate([l0, l1], 1)
        for a in range(2):
            left = slice(a * 256, (a + 1) * 256)
            tile = product(high_ref[:, left], low_ref[:, left], sh, sl)
            for i in range(2):
                for j in range(2):
                    gram_ref[(2 * a + i) * 4 + place_ref[2 * pair + j]] = tile[
                        i * GROUP : (i + 1) * GROUP, j * GROUP : (j + 1) * GROUP
                    ]


VMEM = pl.BlockSpec(memory_space=pltpu.VMEM)
SMEM = pl.BlockSpec(memory_space=pltpu.SMEM)


def local_strips(snapshots, region_ids, conductivity):
    rows, width = region_ids.shape
    nodes = rows * STRIP
    field = snapshots.reshape(rows, width, GROUP)
    h, l, x, y, c = (lax.axis_index(a) for a in ALL)

    seam = jnp.concatenate(
        [field[:, 2 * STRIP], jnp.zeros((SEAM - rows, GROUP), jnp.float32)], 0
    )

    def strip_at(t):
        main = lax.dynamic_slice_in_dim(field, t * STRIP, STRIP, 1).reshape(nodes, GROUP)
        return jnp.concatenate([main, seam], 0)

    far_same = strip_at(2 * (1 - h) + x)
    far_flip = strip_at(2 * (1 - h) + (1 - x))
    near = [lax.ppermute(far_same, ALL, crossing(False, 0)), lax.ppermute(far_flip, ALL, crossing(False, 1))]

    none = jnp.zeros((rows, GROUP), jnp.float32)
    pad = jnp.zeros((8 - rows, GROUP), jnp.float32)
    pieces = []
    for t in (2, 3, 0, 1):
        left = field[:, t * STRIP - 1] if t > 0 else none
        right = field[:, (t + 1) * STRIP] if t < 3 else none
        main = field[:, t * STRIP : (t + 1) * STRIP].reshape(nodes, GROUP)
        pieces.append(jnp.concatenate([main, left, pad, right, pad], 0))
    own = lax.all_to_all(jnp.stack(pieces), PLACE, 0, 0, tiled=True)

    far_same, far_flip, own, *near = lax.optimization_barrier((far_same, far_flip, own, *near))
    far = [lax.ppermute(far_same, ALL, crossing(True, 0)), lax.ppermute(far_flip, ALL, crossing(True, 1))]

    def edge(r):
        return jnp.concatenate(
            [
                own[:, r * STRIP : (r + 1) * STRIP],
                own[:, nodes + r : nodes + r + 1],
                own[:, nodes + 8 + r : nodes + 8 + r + 1],
                jnp.zeros((4, 6, GROUP), jnp.float32),
            ],
            1,
        )

    above = lax.ppermute(edge(rows - 1), TILE, [(m, m + 1) for m in range(3)])
    below = lax.ppermute(edge(0), TILE, [(m + 1, m) for m in range(3)])

    total_nodes = snapshots.shape[0] * 4
    weight = weights_of(region_ids, conductivity) / math.sqrt(total_nodes)
    weight_above = lax.ppermute(weight[rows - 1 :], TILE, [(m, m + 1) for m in range(3)])
    weight = jnp.pad(jnp.concatenate([weight_above, weight], 0), ((0, 0), (8, 8)))
    weight = lax.dynamic_slice_in_dim(weight, (2 * (1 - l) + x) * STRIP, STRIP + 16, 1)
    weight = jnp.broadcast_to(weight[:, :, None], (rows + 1, STRIP + 16, GROUP))

    blocks = jax.ShapeDtypeStruct((16, GROUP, GROUP), jnp.float32)
    half_float = jax.ShapeDtypeStruct((nodes + SEAM, 4 * GROUP), jnp.bfloat16)
    seam_side = jnp.stack([(h == 0) & (x == 1), (h == 1) & (x == 0)]).astype(jnp.float32)
    seam_side = seam_side * jnp.array([1.0, -1.0], jnp.float32)
    high, low, own_blocks = pl.pallas_call(
        lambda *refs: own_kernel(rows, *refs),
        out_shape=(half_float, half_float, blocks),
        in_specs=[SMEM] + [VMEM] * 4,
        out_specs=(VMEM,) * 3,
        scratch_shapes=[pltpu.VMEM((nodes, 4 * GROUP), jnp.bfloat16)] * 2,
        compiler_params=pltpu.CompilerParams(vmem_limit_bytes=40 * 1024 * 1024),
        cost_estimate=pl.CostEstimate(
            flops=6 * nodes * 512 * 512, bytes_accessed=6 * 1024 * 1024, transcendentals=0
        ),
    )(seam_side, own, above, below, weight)

    place = jnp.stack([2 * h + x, 2 * h + (1 - x), 2 * (1 - h) + x, 2 * (1 - h) + (1 - x)])
    cross_blocks = pl.pallas_call(
        cross_kernel,
        out_shape=blocks,
        in_specs=[SMEM] + [VMEM] * 6,
        out_specs=VMEM,
        compiler_params=pltpu.CompilerParams(vmem_limit_bytes=40 * 1024 * 1024),
        cost_estimate=pl.CostEstimate(
            flops=6 * nodes * 512 * 512, bytes_accessed=5 * 1024 * 1024, transcendentals=0
        ),
    )(place.astype(jnp.int32), high, low, *near, *far)

    def gathered(parts):
        return jnp.sum(lax.all_to_all(parts, PLACE + TILE, 0, 0, tiled=True), 0)

    own_block = gathered(own_blocks)
    cross_block = gathered(cross_blocks)
    swap = []
    for half in range(2):
        for i in range(4):
            for m in range(4):
                swap.append((half * 16 + i * 4 + m, (1 - half) * 16 + m * 4 + i))
    cross_block = cross_block + lax.ppermute(cross_block, ALL, swap).T

    first = jnp.where(h == 0, own_block, cross_block)
    last = jnp.where(h == 0, cross_block, own_block)
    one = jnp.where(c == 0, first, last)
    two = jnp.where(c == 0, last, first)
    one = lax.ppermute(one, TILE, [(0, 0), (1, 2), (2, 1), (3, 3)])
    two = lax.ppermute(two, TILE, [(0, 2), (1, 0), (2, 3), (3, 1)])
    return jnp.where(
        y == 0, jnp.concatenate([one, two], 1), jnp.concatenate([two, one], 1)
    )


def solution(mesh):
    sizes = (mesh.shape["snap"], mesh.shape["mesh"])

    def whole(snapshots, region_ids, conductivity):
        width = region_ids.shape[1]
        if sizes == (8, 4) and snapshots.shape[1] == 8 * GROUP and width == 4 * STRIP:
            parts = Mesh(mesh.devices.reshape(2, 2, 2, 2, 2), ALL)
            return jax.shard_map(
                local_strips,
                mesh=parts,
                in_specs=(P(TILE, ("h", "l", "x")), P(TILE, None), P()),
                out_specs=P(("h", "l", "x"), TILE),
                check_vma=False,
            )(snapshots, region_ids, conductivity)
        return jax.shard_map(
            local_ring,
            mesh=mesh,
            in_specs=(P("mesh", "snap"), P("mesh", None), P()),
            out_specs=P("snap", "mesh"),
            check_vma=False,
        )(snapshots, region_ids, conductivity)

    return whole
```

```python
import math

import jax
import jax.numpy as jnp
from jax import lax
from jax.experimental import pallas as pl
from jax.experimental.pallas import tpu as pltpu
from jax.sharding import Mesh
from jax.sharding import PartitionSpec as P


def passed_along(value, axis, steps):
    count = lax.axis_size(axis)
    first, last = (max(0, -steps), min(count, count - steps))
    return lax.ppermute(value, axis, [(source, source + steps) for source in range(first, last)])


def from_behind(block, axis, distance):
    devices = range(lax.axis_size(axis))
    route = [((i - distance) % len(devices), i) for i in devices]
    return lax.ppermute(block, axis, route)


def weights_of(region_ids, conductivity):
    table = jnp.arange(conductivity.shape[0], dtype=jnp.int32)
    picked = jnp.where(
        region_ids[:, :, None] == table[None, None, :],
        conductivity[None, None, :],
        jnp.zeros((), conductivity.dtype),
    )
    return jnp.sum(picked, axis=-1) / 36.0


def element_terms(field, below, weight):
    lower = jnp.concatenate([field, below[None]], 0)
    padded = jnp.pad(lower, ((0, 0), (0, 1), (0, 0)))
    corner_a = padded[:-1, :-1]
    corner_b = padded[:-1, 1:]
    corner_e = padded[1:, :-1]
    corner_d = padded[1:, 1:]
    scaled = weight[:, :, None]
    to_a = scaled * (4.0 * corner_a + 2.0 * corner_b + 2.0 * corner_e + corner_d)
    to_b = scaled * (2.0 * corner_a + 4.0 * corner_b + corner_e + 2.0 * corner_d)
    to_e = scaled * (2.0 * corner_a + corner_b + 4.0 * corner_e + 2.0 * corner_d)
    to_d = scaled * (corner_a + 2.0 * corner_b + 2.0 * corner_e + 4.0 * corner_d)
    total = jnp.pad(to_a, ((0, 1), (0, 1), (0, 0))) + jnp.pad(to_b, ((0, 1), (1, 0), (0, 0)))
    total = (
        total + jnp.pad(to_e, ((1, 0), (0, 1), (0, 0))) + jnp.pad(to_d, ((1, 0), (1, 0), (0, 0)))
    )
    return total


def contract(left, right):
    return lax.dot_general(
        left,
        right,
        (((0,), (0,)), ((), ())),
        precision=lax.Precision.HIGHEST,
        preferred_element_type=jnp.float32,
    )


def local_ring(snapshots, region_ids, conductivity):
    strip, width = region_ids.shape
    node_rows, group_cols = snapshots.shape
    field = snapshots.reshape(strip, width, group_cols)
    weight = weights_of(region_ids, conductivity)
    below = passed_along(field[0], "mesh", -1)
    total = element_terms(field, below, weight)
    carried = passed_along(total[strip, :width], "mesh", 1)
    inner = total[:strip, :width]
    panel = jnp.concatenate([inner[:1] + carried[None], inner[1:]], 0).reshape(
        node_rows, group_cols
    )
    count = lax.axis_size("snap")
    group = lax.axis_index("snap")
    reach = count // 2

    def place(partial_value, moving, step):
        tile = contract(snapshots, moving)
        source = (group - step) % count * group_cols
        return lax.dynamic_update_slice(partial_value, tile, (jnp.int32(0), source))

    partial_value = place(jnp.zeros((group_cols, group_cols * count), jnp.float32), panel, 0)

    def turn(step, carry):
        moving, partial_value = carry
        moving = from_behind(moving, "snap", 1)
        return (moving, place(partial_value, moving, step))

    _, partial_value = lax.fori_loop(1, reach + 1, turn, (panel, partial_value))
    blocks = jnp.transpose(partial_value.reshape(group_cols, count, group_cols), (1, 2, 0))
    target = jnp.arange(count, dtype=jnp.int32)
    offset = (group - target) % count
    valid = (offset >= 1) & (offset <= count - 1 - reach)
    outgoing = jnp.where(valid[:, None, None], blocks, jnp.zeros((), jnp.float32))
    incoming = lax.all_to_all(outgoing, "snap", split_axis=0, concat_axis=0, tiled=True)
    partial_value = partial_value + jnp.transpose(incoming, (1, 0, 2)).reshape(
        group_cols, count * group_cols
    )
    summed = lax.psum_scatter(partial_value, "mesh", scatter_dimension=1, tiled=True)
    total_nodes = node_rows * lax.axis_size("mesh")
    return summed / math.sqrt(total_nodes)


ALL = ("h", "l", "x", "y", "c")
PLACE = ("l", "x")
TILE = ("y", "c")
GROUP = 128
STRIP = 128
SEAM = 16
LAST = 3


def flat(h, l, x, y, c):
    return (((h * 2 + l) * 2 + x) * 2 + y) * 2 + c


def crossing(outer, flip):
    pairs = []
    for h in range(2):
        l = h if outer else 1 - h
        for x in range(2):
            for y in range(2):
                for c in range(2):
                    pairs.append((flat(h, l, x, y, c), flat(1 - h, h, x ^ flip, y, c)))
    return pairs


def middle_groups():
    four = [(x, y) for x in range(2) for y in range(2)]
    groups = [[flat(h, 1 - h, x, y, c) for h in range(2) for x, y in four] for c in range(2)]
    groups += [[flat(h, h, x, y, c) for x, y in four for c in range(2)] for h in range(2)]
    return groups


def owners(turn):
    pairs = []
    for h in range(2):
        for x in range(2):
            for y in range(2):
                for c in range(2):
                    lower = flat(0, h, x, 1, c)
                    upper = flat(1, c, y, 0, h)
                    down = (x + y + turn) % 2 == 0
                    pairs.append((flat(h, 1 - h, x, y, c), lower if down else upper))
    return pairs


MIDDLE_GROUPS = middle_groups()


def split(value):
    high = value.astype(jnp.bfloat16)
    return high, (value - high.astype(jnp.float32)).astype(jnp.bfloat16)


def product(left_high, left_low, right_high, right_low):
    def one(a, b):
        return lax.dot_general(
            a, b, (((0,), (0,)), ((), ())), preferred_element_type=jnp.float32
        )

    return one(left_high, right_high) + one(left_high, right_low) + one(left_low, right_high)


def own_kernel(
    rows,
    side_ref,
    seam_ref,
    field_ref,
    above_ref,
    below_ref,
    weight_ref,
    high_ref,
    low_ref,
    mine_ref,
    other_ref,
    sh,
    sl,
):
    wide = STRIP + 16
    line_number = lax.broadcasted_iota(jnp.int32, (SEAM, GROUP), 0)
    first_core = side_ref[0] == 0
    x, l = side_ref[2], side_ref[3]

    def line(main, left, right):
        return jnp.concatenate(
            [
                jnp.broadcast_to(left, (8, GROUP)),
                main,
                jnp.broadcast_to(right, (8, GROUP)),
            ],
            0,
        )

    def halo(ref, g):
        at = g * (STRIP + 8)
        end = at + STRIP
        return line(ref[at:end], ref[end : end + 1], ref[end + 1 : end + 2])

    body = rows * STRIP
    for g in range(4):
        columns = slice(g * GROUP, (g + 1) * GROUP)
        before = halo(above_ref, g)
        before_up = pltpu.roll(before, wide - 1, 0)
        carried = carried_next = None
        seam = jnp.zeros((SEAM, GROUP), jnp.float32)
        for r in range(-1, rows):
            n = r + 1
            if n < rows:
                main = field_ref[g, n * STRIP : (n + 1) * STRIP]
                after = line(
                    main,
                    field_ref[g, body + n : body + n + 1],
                    field_ref[g, body + 8 + n : body + 9 + n],
                )
                high, low = split(main)
                sh[n * STRIP : (n + 1) * STRIP, columns] = high
                sl[n * STRIP : (n + 1) * STRIP, columns] = low
            else:
                after = halo(below_ref, g)
            after_up = pltpu.roll(after, wide - 1, 0)
            weight = weight_ref[r] if r >= 0 else above_ref[4 * (STRIP + 8) :]
            top, top_up = 2.0 * before + after, 2.0 * before_up + after_up
            to_a, to_b = weight * (2.0 * top + top_up), weight * (top + 2.0 * top_up)
            if r >= 0:
                from_left = pltpu.roll(to_b + carried_next, 1, 0)
                total = to_a + carried + from_left
                beside = (
                    seam_ref[0] * from_left[8 + STRIP : 9 + STRIP] + seam_ref[1] * from_left[8:9]
                )
                seam = jnp.where(line_number == r, beside, seam)
                high, low = split(total[8 : 8 + STRIP])
                high_ref[r * STRIP : (r + 1) * STRIP, columns] = high
                low_ref[r * STRIP : (r + 1) * STRIP, columns] = low
            low_end, low_up = before + 2.0 * after, before_up + 2.0 * after_up
            carried = weight * (2.0 * low_end + low_up)
            carried_next = weight * (low_end + 2.0 * low_up)
            before, before_up = after, after_up
        high, low = split(seam)
        high_ref[body : body + SEAM, columns] = high
        low_ref[body : body + SEAM, columns] = low
    for a in range(2):
        left = slice(a * 256, (a + 1) * 256)
        tiles = [
            product(
                sh[:, left], sl[:, left], high_ref[:body, right], low_ref[:body, right]
            )
            for right in (slice(0, 256), slice(256, 512))
        ]
        mine = jnp.where(first_core, tiles[0], tiles[1])
        other = jnp.where(first_core, tiles[1], tiles[0])
        for i in range(2):
            rows_of = slice(i * GROUP, (i + 1) * GROUP)
            mine_ref[l ^ a, x ^ i] = mine[rows_of]
            other_ref[l ^ a, x ^ i] = other[rows_of]


def cross_kernel(side_ref, high_ref, low_ref, *refs):
    *pieces, mine_ref, other_ref = refs
    core, half, x = side_ref[0], side_ref[1], side_ref[2]

    def put(to_core, slot, block):
        @pl.when(core == to_core)
        def _():
            mine_ref[slot] = block

        @pl.when(core != to_core)
        def _():
            other_ref[slot] = block

    for pair in range(2):
        first, second = (
            jnp.concatenate([pieces[k][...], pieces[k + 1][...]], 0)
            for k in (4 * pair, 4 * pair + 2)
        )
        sh, sl = split(jnp.concatenate([first, second], 1))
        for a in range(2):
            own = slice(a * 256, (a + 1) * 256)

            @pl.when(half == 0)
            def _():
                tile = product(high_ref[:, own], low_ref[:, own], sh, sl)
                for i in range(2):
                    for j in range(2):
                        block = tile[i * GROUP : (i + 1) * GROUP, j * GROUP : (j + 1) * GROUP]
                        put(pair, (2 * a + i) * 2 + (x ^ j), block)

            @pl.when(half == 1)
            def _():
                tile = product(sh, sl, high_ref[:, own], low_ref[:, own])
                for i in range(2):
                    for j in range(2):
                        block = tile[i * GROUP : (i + 1) * GROUP, j * GROUP : (j + 1) * GROUP]
                        put(a, (2 * (1 - pair) + (x ^ i)) * 2 + j, block)


VMEM = pl.BlockSpec(memory_space=pltpu.VMEM)
SMEM = pl.BlockSpec(memory_space=pltpu.SMEM)


def local_strips(snapshots, region_ids, conductivity):
    rows, width = region_ids.shape
    nodes = rows * STRIP
    field = snapshots.reshape(rows, width, GROUP)
    h, l, x, y, c = (lax.axis_index(a) for a in ALL)

    seam = jnp.concatenate(
        [field[:, 2 * STRIP], jnp.zeros((SEAM - rows, GROUP), jnp.float32)], 0
    )

    def strip_at(t):
        main = lax.dynamic_slice_in_dim(field, t * STRIP, STRIP, 1)
        return [
            main[: rows - LAST].reshape(-1, GROUP),
            jnp.concatenate([main[rows - LAST :].reshape(-1, GROUP), seam], 0),
        ]

    far = [[], []]
    for flip in range(2):
        strip = strip_at(2 * (1 - h) + (x ^ flip))
        done = None
        for outer in (False, True):
            for piece in strip:
                if done is not None:
                    piece, done = lax.optimization_barrier((piece, done))
                    far[flip][-1] = done
                done = lax.ppermute(piece, ALL, crossing(outer, flip))
                far[flip].append(done)
    none = jnp.zeros((rows, GROUP), jnp.float32)
    pad = jnp.zeros((8 - rows, GROUP), jnp.float32)
    pieces = []
    for t in (2, 3, 0, 1):
        left = field[:, t * STRIP - 1] if t > 0 else none
        right = field[:, (t + 1) * STRIP] if t < 3 else none
        main = field[:, t * STRIP : (t + 1) * STRIP].reshape(nodes, GROUP)
        pieces.append(jnp.concatenate([main, left, pad, right, pad], 0))
    strips = lax.all_to_all(jnp.stack(pieces), PLACE, 0, 0, tiled=True)

    total_nodes = snapshots.shape[0] * 4
    weight = weights_of(region_ids, conductivity) / math.sqrt(total_nodes)
    weight = jnp.pad(weight, ((0, 0), (8, 8)))
    weight = lax.dynamic_slice_in_dim(weight, (2 * (1 - l) + x) * STRIP, STRIP + 16, 1)
    weight = jnp.broadcast_to(weight[:, :, None], (rows, STRIP + 16, GROUP))

    def edge(r):
        return jnp.concatenate(
            [
                strips[:, r * STRIP : (r + 1) * STRIP],
                strips[:, nodes + r : nodes + r + 1],
                strips[:, nodes + 8 + r : nodes + 9 + r],
                jnp.zeros((4, 6, GROUP), jnp.float32),
            ],
            1,
        ).reshape(4 * (STRIP + 8), GROUP)

    above = jnp.concatenate([edge(rows - 1), weight[rows - 1]], 0)
    below = edge(0)
    above = lax.ppermute(above, TILE, [(m, m + 1) for m in range(3)])
    below = lax.ppermute(below, TILE, [(m + 1, m) for m in range(3)])
    far = [far[flip][2 * outer + k] for outer in range(2) for flip in range(2) for k in range(2)]

    side = jnp.stack([c, h, x, l]).astype(jnp.int32)
    seam_side = jnp.stack([(h == 0) & (x == 1), (h == 1) & (x == 0)]).astype(jnp.float32)
    seam_side = seam_side * jnp.array([1.0, -1.0], jnp.float32)
    blocks = jax.ShapeDtypeStruct((8, GROUP, GROUP), jnp.float32)
    own_blocks = jax.ShapeDtypeStruct((2, 2, GROUP, 2 * GROUP), jnp.float32)
    half_float = jax.ShapeDtypeStruct((nodes + SEAM, 4 * GROUP), jnp.bfloat16)
    high, low, own_mine, own_other = pl.pallas_call(
        lambda *refs: own_kernel(rows, *refs),
        out_shape=(half_float, half_float, own_blocks, own_blocks),
        in_specs=[SMEM] * 2 + [VMEM] * 4,
        out_specs=(VMEM,) * 4,
        scratch_shapes=[pltpu.VMEM((nodes, 4 * GROUP), jnp.bfloat16)] * 2,
        compiler_params=pltpu.CompilerParams(vmem_limit_bytes=40 * 1024 * 1024),
        cost_estimate=pl.CostEstimate(flops=1, bytes_accessed=1, transcendentals=0),
    )(side, seam_side, strips, above, below, weight)

    def both_cores(mine, other):
        return mine + lax.ppermute(other, "c", [(0, 1), (1, 0)])

    own = both_cores(own_mine, own_other)
    cross_mine, cross_other = pl.pallas_call(
        cross_kernel,
        out_shape=(blocks, blocks),
        in_specs=[SMEM] + [VMEM] * 10,
        out_specs=(VMEM,) * 2,
        compiler_params=pltpu.CompilerParams(vmem_limit_bytes=40 * 1024 * 1024),
        cost_estimate=pl.CostEstimate(flops=10**11, bytes_accessed=1, transcendentals=0),
    )(side, high, low, *far)

    own, cross_mine, cross_other = lax.optimization_barrier((own, cross_mine, cross_other))
    own = own[0] + lax.ppermute(own[1], "l", [(0, 1), (1, 0)])
    own = own[0] + lax.ppermute(own[1], "x", [(0, 1), (1, 0)])
    to_holder = [
        (flat(i, j, k, 1 - i, n), flat(i, j, k, i, n))
        for i in range(2)
        for j in range(2)
        for k in range(2)
        for n in range(2)
    ]
    own = own + lax.ppermute(own, ALL, to_holder)

    cross = lax.all_to_all(
        both_cores(cross_mine, cross_other), ALL, 0, 0, tiled=True, axis_index_groups=MIDDLE_GROUPS
    )
    cross = jnp.sum(cross, 0)
    even = (x + y) % 2 == 0
    turned = cross.T
    cross_pair = [
        lax.ppermute(jnp.where(even, cross, turned), ALL, owners(0)),
        lax.ppermute(jnp.where(even, turned, cross), ALL, owners(1)),
    ]
    swapped = (x + h) % 2 == 1
    left = jnp.where(swapped, cross_pair[1], cross_pair[0])
    right = jnp.where(swapped, cross_pair[0], cross_pair[1])
    return jnp.where(y == h, own, jnp.concatenate([left, right], 1))


def solution(mesh):
    sizes = (mesh.shape["snap"], mesh.shape["mesh"])

    def whole(snapshots, region_ids, conductivity):
        width = region_ids.shape[1]
        if sizes == (8, 4) and snapshots.shape[1] == 8 * GROUP and width == 4 * STRIP:
            parts = Mesh(mesh.devices.reshape(2, 2, 2, 2, 2), ALL)
            return jax.shard_map(
                local_strips,
                mesh=parts,
                in_specs=(P(TILE, ("h", "l", "x")), P(TILE, None), P()),
                out_specs=P(("h", "l", "x"), TILE),
                check_vma=False,
            )(snapshots, region_ids, conductivity)
        return jax.shard_map(
            local_ring,
            mesh=mesh,
            in_specs=(P("mesh", "snap"), P("mesh", None), P()),
            out_specs=P("snap", "mesh"),
            check_vma=False,
        )(snapshots, region_ids, conductivity)

    return whole
```

```python
import math

import jax
import jax.numpy as jnp
from jax import lax
from jax.experimental import pallas as pl
from jax.experimental.pallas import tpu as pltpu
from jax.sharding import Mesh
from jax.sharding import PartitionSpec as P


def passed_along(value, axis, steps):
    count = lax.axis_size(axis)
    first, last = (max(0, -steps), min(count, count - steps))
    return lax.ppermute(value, axis, [(source, source + steps) for source in range(first, last)])


def from_behind(block, axis, distance):
    devices = range(lax.axis_size(axis))
    route = [((i - distance) % len(devices), i) for i in devices]
    return lax.ppermute(block, axis, route)


def weights_of(region_ids, conductivity):
    table = jnp.arange(conductivity.shape[0], dtype=jnp.int32)
    picked = jnp.where(
        region_ids[:, :, None] == table[None, None, :],
        conductivity[None, None, :],
        jnp.zeros((), conductivity.dtype),
    )
    return jnp.sum(picked, axis=-1) / 36.0


def element_terms(field, below, weight):
    lower = jnp.concatenate([field, below[None]], 0)
    padded = jnp.pad(lower, ((0, 0), (0, 1), (0, 0)))
    corner_a = padded[:-1, :-1]
    corner_b = padded[:-1, 1:]
    corner_e = padded[1:, :-1]
    corner_d = padded[1:, 1:]
    scaled = weight[:, :, None]
    to_a = scaled * (4.0 * corner_a + 2.0 * corner_b + 2.0 * corner_e + corner_d)
    to_b = scaled * (2.0 * corner_a + 4.0 * corner_b + corner_e + 2.0 * corner_d)
    to_e = scaled * (2.0 * corner_a + corner_b + 4.0 * corner_e + 2.0 * corner_d)
    to_d = scaled * (corner_a + 2.0 * corner_b + 2.0 * corner_e + 4.0 * corner_d)
    total = jnp.pad(to_a, ((0, 1), (0, 1), (0, 0))) + jnp.pad(to_b, ((0, 1), (1, 0), (0, 0)))
    total = (
        total + jnp.pad(to_e, ((1, 0), (0, 1), (0, 0))) + jnp.pad(to_d, ((1, 0), (1, 0), (0, 0)))
    )
    return total


def contract(left, right):
    return lax.dot_general(
        left,
        right,
        (((0,), (0,)), ((), ())),
        precision=lax.Precision.HIGHEST,
        preferred_element_type=jnp.float32,
    )


def local_ring(snapshots, region_ids, conductivity):
    strip, width = region_ids.shape
    node_rows, group_cols = snapshots.shape
    field = snapshots.reshape(strip, width, group_cols)
    weight = weights_of(region_ids, conductivity)
    below = passed_along(field[0], "mesh", -1)
    total = element_terms(field, below, weight)
    carried = passed_along(total[strip, :width], "mesh", 1)
    inner = total[:strip, :width]
    panel = jnp.concatenate([inner[:1] + carried[None], inner[1:]], 0).reshape(
        node_rows, group_cols
    )
    count = lax.axis_size("snap")
    group = lax.axis_index("snap")
    reach = count // 2

    def place(partial_value, moving, step):
        tile = contract(snapshots, moving)
        source = (group - step) % count * group_cols
        return lax.dynamic_update_slice(partial_value, tile, (jnp.int32(0), source))

    partial_value = place(jnp.zeros((group_cols, group_cols * count), jnp.float32), panel, 0)

    def turn(step, carry):
        moving, partial_value = carry
        moving = from_behind(moving, "snap", 1)
        return (moving, place(partial_value, moving, step))

    _, partial_value = lax.fori_loop(1, reach + 1, turn, (panel, partial_value))
    blocks = jnp.transpose(partial_value.reshape(group_cols, count, group_cols), (1, 2, 0))
    target = jnp.arange(count, dtype=jnp.int32)
    offset = (group - target) % count
    valid = (offset >= 1) & (offset <= count - 1 - reach)
    outgoing = jnp.where(valid[:, None, None], blocks, jnp.zeros((), jnp.float32))
    incoming = lax.all_to_all(outgoing, "snap", split_axis=0, concat_axis=0, tiled=True)
    partial_value = partial_value + jnp.transpose(incoming, (1, 0, 2)).reshape(
        group_cols, count * group_cols
    )
    summed = lax.psum_scatter(partial_value, "mesh", scatter_dimension=1, tiled=True)
    total_nodes = node_rows * lax.axis_size("mesh")
    return summed / math.sqrt(total_nodes)


ALL = ("h", "l", "x", "y", "c")
PLACE = ("l", "x")
TILE = ("y", "c")
GROUP = 128
STRIP = 128
SEAM = 16


def flat(h, l, x, y, c):
    return (((h * 2 + l) * 2 + x) * 2 + y) * 2 + c


def crossing(outer, flip):
    pairs = []
    for h in range(2):
        l = h if outer else 1 - h
        for x in range(2):
            for y in range(2):
                for c in range(2):
                    pairs.append((flat(h, l, x, y, c), flat(1 - h, h, x ^ flip, y, c)))
    return pairs


def middle_groups():
    four = [(x, y) for x in range(2) for y in range(2)]
    groups = [[flat(h, 1 - h, x, y, c) for h in range(2) for x, y in four] for c in range(2)]
    groups += [[flat(h, h, x, y, c) for x, y in four for c in range(2)] for h in range(2)]
    return groups


def owners(turn):
    pairs = []
    for h in range(2):
        for x in range(2):
            for y in range(2):
                for c in range(2):
                    lower = flat(0, h, x, 1, c)
                    upper = flat(1, c, y, 0, h)
                    down = (x + y + turn) % 2 == 0
                    pairs.append((flat(h, 1 - h, x, y, c), lower if down else upper))
    return pairs


MIDDLE_GROUPS = middle_groups()


def split(value):
    high = value.astype(jnp.bfloat16)
    return high, (value - high.astype(jnp.float32)).astype(jnp.bfloat16)


def product(left_high, left_low, right_high, right_low, turned=False):
    def one(a, b):
        return lax.dot_general(
            a, b, (((1 if turned else 0,), (0,)), ((), ())), preferred_element_type=jnp.float32
        )

    return one(left_high, right_high) + one(left_high, right_low) + one(left_low, right_high)


def own_kernel(
    rows,
    side_ref,
    seam_ref,
    ends_ref,
    field_ref,
    above_ref,
    below_ref,
    weight_ref,
    high_ref,
    low_ref,
    mine_ref,
    other_ref,
    sh,
    sl,
    ph,
    pw,
):
    wide = STRIP + 16
    line_number = lax.broadcasted_iota(jnp.int32, (SEAM, GROUP), 0)
    first_core = side_ref[0] == 0
    x, l = side_ref[2], side_ref[3]

    def line(main, left, right):
        return jnp.concatenate(
            [
                jnp.broadcast_to(left, (8, GROUP)),
                main,
                jnp.broadcast_to(right, (8, GROUP)),
            ],
            0,
        )

    def halo(ref, g):
        at = g * (STRIP + 8)
        end = at + STRIP
        return line(ref[at:end], ref[end : end + 1], ref[end + 1 : end + 2])

    body = rows * STRIP
    for g in range(4):
        columns = slice(g * GROUP, (g + 1) * GROUP)
        before = halo(above_ref, g)
        before_up = pltpu.roll(before, wide - 1, 0)
        carried = carried_next = None
        seam = jnp.zeros((SEAM, GROUP), jnp.float32)
        for r in range(-1, rows):
            n = r + 1
            if n < rows:
                if n in (0, rows - 1):
                    at = 0 if n == 0 else STRIP
                    main = ends_ref[g, at : at + STRIP]
                else:
                    main = field_ref[g, (n - 1) * STRIP : n * STRIP]
                sides = 2 * STRIP + n
                after = line(
                    main,
                    ends_ref[g, sides : sides + 1],
                    ends_ref[g, sides + 8 : sides + 9],
                )
                high, low = split(main)
                sh[n * STRIP : (n + 1) * STRIP, columns] = high
                sl[n * STRIP : (n + 1) * STRIP, columns] = low
            else:
                after = halo(below_ref, g)
            after_up = pltpu.roll(after, wide - 1, 0)
            weight = weight_ref[r] if r >= 0 else above_ref[4 * (STRIP + 8) :]
            top, top_up = 2.0 * before + after, 2.0 * before_up + after_up
            to_a, to_b = weight * (2.0 * top + top_up), weight * (top + 2.0 * top_up)
            if r >= 0:
                from_left = pltpu.roll(to_b + carried_next, 1, 0)
                total = to_a + carried + from_left
                beside = (
                    seam_ref[0] * from_left[8 + STRIP : 9 + STRIP] + seam_ref[1] * from_left[8:9]
                )
                seam = jnp.where(line_number == r, beside, seam)
                high, low = split(total[8 : 8 + STRIP])
                ph[r * STRIP : (r + 1) * STRIP, columns] = high
                pw[r * STRIP : (r + 1) * STRIP, columns] = low
            low_end, low_up = before + 2.0 * after, before_up + 2.0 * after_up
            carried = weight * (2.0 * low_end + low_up)
            carried_next = weight * (low_end + 2.0 * low_up)
            before, before_up = after, after_up
        high, low = split(seam)
        ph[body : body + SEAM, columns] = high
        pw[body : body + SEAM, columns] = low
    for a in range(2):
        left = slice(a * 256, (a + 1) * 256)
        tiles = [
            product(
                sh[:, left], sl[:, left], ph[:body, right], pw[:body, right]
            )
            for right in (slice(0, 256), slice(256, 512))
        ]
        mine = jnp.where(first_core, tiles[0], tiles[1])
        other = jnp.where(first_core, tiles[1], tiles[0])
        for i in range(2):
            rows_of = slice(i * GROUP, (i + 1) * GROUP)
            mine_ref[l ^ a, x ^ i] = mine[rows_of]
            other_ref[l ^ a, x ^ i] = other[rows_of]
    for turned_ref, panel in ((high_ref, ph), (low_ref, pw)):
        turned_ref[...] = panel[...].T


def cross_kernel(side_ref, high_ref, low_ref, s0, s1, s2, s3, mine_ref, other_ref, tiles):
    core, half, x = side_ref[0], side_ref[1], side_ref[2]
    for pair, (first, second) in enumerate(((s0, s1), (s2, s3))):
        h0, l0 = split(first[...])
        h1, l1 = split(second[...])
        sh = jnp.concatenate([h0, h1], 1)
        sl = jnp.concatenate([l0, l1], 1)
        for a in range(2):
            own = slice(a * 256, (a + 1) * 256)
            tiles[pair, a] = product(high_ref[own], low_ref[own], sh, sl, turned=True)

    def place(h, c):
        for pair in range(2):
            for a in range(2):
                ref = mine_ref if (a if h else pair) == c else other_ref
                for i in range(2):
                    for j in range(2):
                        block = tiles[
                            pair, a, i * GROUP : (i + 1) * GROUP, j * GROUP : (j + 1) * GROUP
                        ]
                        if h:
                            ref[(2 * (1 - pair) + (x ^ j)) * 2 + i] = block.T
                        else:
                            ref[(2 * a + i) * 2 + (x ^ j)] = block

    for h in range(2):
        for c in range(2):
            pl.when((half == h) & (core == c))(lambda: place(h, c))


VMEM = pl.BlockSpec(memory_space=pltpu.VMEM)
SMEM = pl.BlockSpec(memory_space=pltpu.SMEM)


def local_strips(snapshots, region_ids, conductivity):
    rows, width = region_ids.shape
    nodes = rows * STRIP
    field = snapshots.reshape(rows, width, GROUP)
    h, l, x, y, c = (lax.axis_index(a) for a in ALL)

    seam = jnp.concatenate(
        [field[:, 2 * STRIP], jnp.zeros((SEAM - rows, GROUP), jnp.float32)], 0
    )

    def strip_at(t):
        main = lax.dynamic_slice_in_dim(field, t * STRIP, STRIP, 1)
        return [jnp.concatenate([main.reshape(nodes, GROUP), seam], 0)]

    halves = [strip_at(2 * (1 - h) + (x ^ flip))[0] for flip in range(2)]
    near = [lax.ppermute(halves[0], ALL, crossing(False, 0))]

    none = jnp.zeros((rows, GROUP), jnp.float32)
    pad = jnp.zeros((8 - rows, GROUP), jnp.float32)
    ends, between = [], []
    for t in (2, 3, 0, 1):
        left = field[:, t * STRIP - 1] if t > 0 else none
        right = field[:, (t + 1) * STRIP] if t < 3 else none
        main = field[:, t * STRIP : (t + 1) * STRIP]
        ends.append(jnp.concatenate([main[0], main[rows - 1], left, pad, right, pad], 0))
        between.append(main[1 : rows - 1].reshape((rows - 2) * STRIP, GROUP))
    ends = lax.all_to_all(jnp.stack(ends), PLACE, 0, 0, tiled=True)
    between = lax.all_to_all(jnp.stack(between), PLACE, 0, 0, tiled=True)
    half, ends = lax.optimization_barrier((halves[1], ends))
    near.append(lax.ppermute(half, ALL, crossing(False, 1)))

    total_nodes = snapshots.shape[0] * 4
    weight = weights_of(region_ids, conductivity) / math.sqrt(total_nodes)
    weight = jnp.pad(weight, ((0, 0), (8, 8)))
    weight = lax.dynamic_slice_in_dim(weight, (2 * (1 - l) + x) * STRIP, STRIP + 16, 1)
    weight = jnp.broadcast_to(weight[:, :, None], (rows, STRIP + 16, GROUP))

    def edge(at, r):
        return jnp.concatenate(
            [
                ends[:, at : at + STRIP],
                ends[:, 2 * STRIP + r : 2 * STRIP + r + 1],
                ends[:, 2 * STRIP + 8 + r : 2 * STRIP + 9 + r],
                jnp.zeros((4, 6, GROUP), jnp.float32),
            ],
            1,
        ).reshape(4 * (STRIP + 8), GROUP)

    above = jnp.concatenate([edge(STRIP, rows - 1), weight[rows - 1]], 0)
    below = edge(0, 0)
    above = lax.ppermute(above, TILE, [(m, m + 1) for m in range(3)])
    below = lax.ppermute(below, TILE, [(m + 1, m) for m in range(3)])
    far = []
    for flip in range(2):
        half, near[flip], above, below = lax.optimization_barrier(
            (halves[flip], near[flip], above, below)
        )
        far.append(lax.ppermute(half, ALL, crossing(True, flip)))

    side = jnp.stack([c, h, x, l]).astype(jnp.int32)
    seam_side = jnp.stack([(h == 0) & (x == 1), (h == 1) & (x == 0)]).astype(jnp.float32)
    seam_side = seam_side * jnp.array([1.0, -1.0], jnp.float32)
    blocks = jax.ShapeDtypeStruct((8, GROUP, GROUP), jnp.float32)
    own_blocks = jax.ShapeDtypeStruct((2, 2, GROUP, 2 * GROUP), jnp.float32)
    half_float = jax.ShapeDtypeStruct((4 * GROUP, nodes + SEAM), jnp.bfloat16)
    high, low, own_mine, own_other = pl.pallas_call(
        lambda *refs: own_kernel(rows, *refs),
        out_shape=(half_float, half_float, own_blocks, own_blocks),
        in_specs=[SMEM] * 2 + [VMEM] * 5,
        out_specs=(VMEM,) * 4,
        scratch_shapes=[pltpu.VMEM((nodes, 4 * GROUP), jnp.bfloat16)] * 2
        + [pltpu.VMEM((nodes + SEAM, 4 * GROUP), jnp.bfloat16)] * 2,
        compiler_params=pltpu.CompilerParams(vmem_limit_bytes=40 * 1024 * 1024),
        cost_estimate=pl.CostEstimate(flops=1, bytes_accessed=1, transcendentals=0),
    )(side, seam_side, ends, between, above, below, weight)

    def both_cores(mine, other):
        return mine + lax.ppermute(other, "c", [(0, 1), (1, 0)])

    own = both_cores(own_mine, own_other)
    cross_mine, cross_other = pl.pallas_call(
        cross_kernel,
        out_shape=(blocks, blocks),
        in_specs=[SMEM] + [VMEM] * 6,
        out_specs=(VMEM,) * 2,
        scratch_shapes=[pltpu.VMEM((2, 2, 256, 256), jnp.float32)],
        compiler_params=pltpu.CompilerParams(vmem_limit_bytes=40 * 1024 * 1024),
        cost_estimate=pl.CostEstimate(flops=10**11, bytes_accessed=1, transcendentals=0),
    )(side, high, low, *near, *far)

    cross = both_cores(cross_mine, cross_other)
    own, cross = lax.optimization_barrier((own, cross))
    own = own[0] + lax.ppermute(own[1], "l", [(0, 1), (1, 0)])
    own = own[0] + lax.ppermute(own[1], "x", [(0, 1), (1, 0)])
    to_holder = [
        (flat(i, j, k, 1 - i, n), flat(i, j, k, i, n))
        for i in range(2)
        for j in range(2)
        for k in range(2)
        for n in range(2)
    ]
    own = own + lax.ppermute(own, ALL, to_holder)

    cross = lax.all_to_all(cross, ALL, 0, 0, tiled=True, axis_index_groups=MIDDLE_GROUPS)
    cross = jnp.sum(cross, 0)
    even = (x + y) % 2 == 0
    turned = cross.T
    cross_pair = [
        lax.ppermute(jnp.where(even, cross, turned), ALL, owners(0)),
        lax.ppermute(jnp.where(even, turned, cross), ALL, owners(1)),
    ]
    swapped = (x + h) % 2 == 1
    left = jnp.where(swapped, cross_pair[1], cross_pair[0])
    right = jnp.where(swapped, cross_pair[0], cross_pair[1])
    return jnp.where(y == h, own, jnp.concatenate([left, right], 1))


def solution(mesh):
    sizes = (mesh.shape["snap"], mesh.shape["mesh"])

    def whole(snapshots, region_ids, conductivity):
        width = region_ids.shape[1]
        if sizes == (8, 4) and snapshots.shape[1] == 8 * GROUP and width == 4 * STRIP:
            parts = Mesh(mesh.devices.reshape(2, 2, 2, 2, 2), ALL)
            return jax.shard_map(
                local_strips,
                mesh=parts,
                in_specs=(P(TILE, ("h", "l", "x")), P(TILE, None), P()),
                out_specs=P(("h", "l", "x"), TILE),
                check_vma=False,
            )(snapshots, region_ids, conductivity)
        return jax.shard_map(
            local_ring,
            mesh=mesh,
            in_specs=(P("mesh", "snap"), P("mesh", None), P()),
            out_specs=P("snap", "mesh"),
            check_vma=False,
        )(snapshots, region_ids, conductivity)

    return whole
```

```python
import math

import jax
import jax.numpy as jnp
from jax import lax
from jax.experimental import pallas as pl
from jax.experimental.pallas import tpu as pltpu
from jax.sharding import Mesh
from jax.sharding import PartitionSpec as P


def passed_along(value, axis, steps):
    count = lax.axis_size(axis)
    first, last = (max(0, -steps), min(count, count - steps))
    return lax.ppermute(value, axis, [(source, source + steps) for source in range(first, last)])


def from_behind(block, axis, distance):
    devices = range(lax.axis_size(axis))
    route = [((i - distance) % len(devices), i) for i in devices]
    return lax.ppermute(block, axis, route)


def weights_of(region_ids, conductivity):
    table = jnp.arange(conductivity.shape[0], dtype=jnp.int32)
    picked = jnp.where(
        region_ids[:, :, None] == table[None, None, :],
        conductivity[None, None, :],
        jnp.zeros((), conductivity.dtype),
    )
    return jnp.sum(picked, axis=-1) / 36.0


def element_terms(field, below, weight):
    lower = jnp.concatenate([field, below[None]], 0)
    padded = jnp.pad(lower, ((0, 0), (0, 1), (0, 0)))
    corner_a = padded[:-1, :-1]
    corner_b = padded[:-1, 1:]
    corner_e = padded[1:, :-1]
    corner_d = padded[1:, 1:]
    scaled = weight[:, :, None]
    to_a = scaled * (4.0 * corner_a + 2.0 * corner_b + 2.0 * corner_e + corner_d)
    to_b = scaled * (2.0 * corner_a + 4.0 * corner_b + corner_e + 2.0 * corner_d)
    to_e = scaled * (2.0 * corner_a + corner_b + 4.0 * corner_e + 2.0 * corner_d)
    to_d = scaled * (corner_a + 2.0 * corner_b + 2.0 * corner_e + 4.0 * corner_d)
    total = jnp.pad(to_a, ((0, 1), (0, 1), (0, 0))) + jnp.pad(to_b, ((0, 1), (1, 0), (0, 0)))
    total = (
        total + jnp.pad(to_e, ((1, 0), (0, 1), (0, 0))) + jnp.pad(to_d, ((1, 0), (1, 0), (0, 0)))
    )
    return total


def contract(left, right):
    return lax.dot_general(
        left,
        right,
        (((0,), (0,)), ((), ())),
        precision=lax.Precision.HIGHEST,
        preferred_element_type=jnp.float32,
    )


def local_ring(snapshots, region_ids, conductivity):
    strip, width = region_ids.shape
    node_rows, group_cols = snapshots.shape
    field = snapshots.reshape(strip, width, group_cols)
    weight = weights_of(region_ids, conductivity)
    below = passed_along(field[0], "mesh", -1)
    total = element_terms(field, below, weight)
    carried = passed_along(total[strip, :width], "mesh", 1)
    inner = total[:strip, :width]
    panel = jnp.concatenate([inner[:1] + carried[None], inner[1:]], 0).reshape(
        node_rows, group_cols
    )
    count = lax.axis_size("snap")
    group = lax.axis_index("snap")
    reach = count // 2

    def place(partial_value, moving, step):
        tile = contract(snapshots, moving)
        source = (group - step) % count * group_cols
        return lax.dynamic_update_slice(partial_value, tile, (jnp.int32(0), source))

    partial_value = place(jnp.zeros((group_cols, group_cols * count), jnp.float32), panel, 0)

    def turn(step, carry):
        moving, partial_value = carry
        moving = from_behind(moving, "snap", 1)
        return (moving, place(partial_value, moving, step))

    _, partial_value = lax.fori_loop(1, reach + 1, turn, (panel, partial_value))
    blocks = jnp.transpose(partial_value.reshape(group_cols, count, group_cols), (1, 2, 0))
    target = jnp.arange(count, dtype=jnp.int32)
    offset = (group - target) % count
    valid = (offset >= 1) & (offset <= count - 1 - reach)
    outgoing = jnp.where(valid[:, None, None], blocks, jnp.zeros((), jnp.float32))
    incoming = lax.all_to_all(outgoing, "snap", split_axis=0, concat_axis=0, tiled=True)
    partial_value = partial_value + jnp.transpose(incoming, (1, 0, 2)).reshape(
        group_cols, count * group_cols
    )
    summed = lax.psum_scatter(partial_value, "mesh", scatter_dimension=1, tiled=True)
    total_nodes = node_rows * lax.axis_size("mesh")
    return summed / math.sqrt(total_nodes)


ALL = ("h", "l", "x", "y", "c")
PLACE = ("l", "x")
TILE = ("y", "c")
GROUP = 128
STRIP = 128
SEAM = 16


def flat(h, l, x, y, c):
    return (((h * 2 + l) * 2 + x) * 2 + y) * 2 + c


def crossing(outer, flip):
    pairs = []
    for h in range(2):
        l = h if outer else 1 - h
        for x in range(2):
            for y in range(2):
                for c in range(2):
                    pairs.append((flat(h, l, x, y, c), flat(1 - h, h, x ^ flip, y, c)))
    return pairs


def middle_groups():
    four = [(x, y) for x in range(2) for y in range(2)]
    groups = [[flat(h, 1 - h, x, y, c) for h in range(2) for x, y in four] for c in range(2)]
    groups += [[flat(h, h, x, y, c) for x, y in four for c in range(2)] for h in range(2)]
    return groups


def owners(turn):
    pairs = []
    for h in range(2):
        for x in range(2):
            for y in range(2):
                for c in range(2):
                    lower = flat(0, h, x, 1, c)
                    upper = flat(1, c, y, 0, h)
                    down = (x + y + turn) % 2 == 0
                    pairs.append((flat(h, 1 - h, x, y, c), lower if down else upper))
    return pairs


MIDDLE_GROUPS = middle_groups()


def split(value):
    high = value.astype(jnp.bfloat16)
    return high, (value - high.astype(jnp.float32)).astype(jnp.bfloat16)


def product(left_high, left_low, right_high, right_low, turned=False):
    def one(a, b):
        return lax.dot_general(
            a, b, (((1 if turned else 0,), (0,)), ((), ())), preferred_element_type=jnp.float32
        )

    return one(left_high, right_high) + one(left_high, right_low) + one(left_low, right_high)


def own_kernel(
    rows,
    side_ref,
    seam_ref,
    ends_ref,
    field_ref,
    above_ref,
    below_ref,
    weight_ref,
    high_ref,
    low_ref,
    mine_ref,
    other_ref,
    sh,
    sl,
    ph,
    pw,
):
    wide = STRIP + 16
    line_number = lax.broadcasted_iota(jnp.int32, (SEAM, GROUP), 0)
    first_core = side_ref[0] == 0
    x, l = side_ref[2], side_ref[3]

    def line(main, left, right):
        return jnp.concatenate(
            [
                jnp.broadcast_to(left, (8, GROUP)),
                main,
                jnp.broadcast_to(right, (8, GROUP)),
            ],
            0,
        )

    def halo(ref, g):
        at = g * (STRIP + 8)
        end = at + STRIP
        return line(ref[at:end], ref[end : end + 1], ref[end + 1 : end + 2])

    body = rows * STRIP
    for g in range(4):
        columns = slice(g * GROUP, (g + 1) * GROUP)
        before = halo(above_ref, g)
        before_up = pltpu.roll(before, wide - 1, 0)
        carried = carried_next = None
        seam = jnp.zeros((SEAM, GROUP), jnp.float32)
        for r in range(-1, rows):
            n = r + 1
            if n < rows:
                if n in (0, rows - 1):
                    at = 0 if n == 0 else STRIP
                    main = ends_ref[g, at : at + STRIP]
                else:
                    main = field_ref[g, (n - 1) * STRIP : n * STRIP]
                sides = 2 * STRIP + n
                after = line(
                    main,
                    ends_ref[g, sides : sides + 1],
                    ends_ref[g, sides + 8 : sides + 9],
                )
                high, low = split(main)
                sh[n * STRIP : (n + 1) * STRIP, columns] = high
                sl[n * STRIP : (n + 1) * STRIP, columns] = low
            else:
                after = halo(below_ref, g)
            after_up = pltpu.roll(after, wide - 1, 0)
            weight = weight_ref[r] if r >= 0 else above_ref[4 * (STRIP + 8) :]
            top, top_up = 2.0 * before + after, 2.0 * before_up + after_up
            to_a, to_b = weight * (2.0 * top + top_up), weight * (top + 2.0 * top_up)
            if r >= 0:
                from_left = pltpu.roll(to_b + carried_next, 1, 0)
                total = to_a + carried + from_left
                beside = (
                    seam_ref[0] * from_left[8 + STRIP : 9 + STRIP] + seam_ref[1] * from_left[8:9]
                )
                seam = jnp.where(line_number == r, beside, seam)
                high, low = split(total[8 : 8 + STRIP])
                ph[r * STRIP : (r + 1) * STRIP, columns] = high
                pw[r * STRIP : (r + 1) * STRIP, columns] = low
            low_end, low_up = before + 2.0 * after, before_up + 2.0 * after_up
            carried = weight * (2.0 * low_end + low_up)
            carried_next = weight * (low_end + 2.0 * low_up)
            before, before_up = after, after_up
        high, low = split(seam)
        ph[body : body + SEAM, columns] = high
        pw[body : body + SEAM, columns] = low
    for a in range(2):
        left = slice(a * 256, (a + 1) * 256)
        tiles = [
            product(
                sh[:, left], sl[:, left], ph[:body, right], pw[:body, right]
            )
            for right in (slice(0, 256), slice(256, 512))
        ]
        mine = jnp.where(first_core, tiles[0], tiles[1])
        other = jnp.where(first_core, tiles[1], tiles[0])
        for i in range(2):
            rows_of = slice(i * GROUP, (i + 1) * GROUP)
            mine_ref[l ^ a, x ^ i] = mine[rows_of]
            other_ref[l ^ a, x ^ i] = other[rows_of]
    for turned_ref, panel in ((high_ref, ph), (low_ref, pw)):
        turned_ref[...] = panel[...].T


def early_kernel(high_ref, low_ref, s0, s1, s2, pair_ref, third_ref):
    h0, l0 = split(s0[...])
    h1, l1 = split(s1[...])
    sh = jnp.concatenate([h0, h1], 1)
    sl = jnp.concatenate([l0, l1], 1)
    pair_ref[...] = product(high_ref[...], low_ref[...], sh, sl, turned=True)
    sh, sl = split(s2[...])
    third_ref[...] = product(high_ref[...], low_ref[...], sh, sl, turned=True)


def cross_kernel(side_ref, high_ref, low_ref, last, pair_ref, third_ref, mine_ref, other_ref, fourth):
    core, half, x = side_ref[0], side_ref[1], side_ref[2]
    sh, sl = split(last[...])
    fourth[...] = product(high_ref[...], low_ref[...], sh, sl, turned=True)

    def place(h, c):
        for pair in range(2):
            for a in range(2):
                ref = mine_ref if (a if h else pair) == c else other_ref
                for i in range(2):
                    for j in range(2):
                        rows_of = slice((2 * a + i) * GROUP, (2 * a + i + 1) * GROUP)
                        if pair == 0:
                            block = pair_ref[rows_of, j * GROUP : (j + 1) * GROUP]
                        else:
                            block = (fourth if j else third_ref)[rows_of]
                        if h:
                            ref[(2 * (1 - pair) + (x ^ j)) * 2 + i] = block.T
                        else:
                            ref[(2 * a + i) * 2 + (x ^ j)] = block

    for h in range(2):
        for c in range(2):
            pl.when((half == h) & (core == c))(lambda: place(h, c))


VMEM = pl.BlockSpec(memory_space=pltpu.VMEM)
SMEM = pl.BlockSpec(memory_space=pltpu.SMEM)


def local_strips(snapshots, region_ids, conductivity):
    rows, width = region_ids.shape
    nodes = rows * STRIP
    field = snapshots.reshape(rows, width, GROUP)
    h, l, x, y, c = (lax.axis_index(a) for a in ALL)

    seam = jnp.concatenate(
        [field[:, 2 * STRIP], jnp.zeros((SEAM - rows, GROUP), jnp.float32)], 0
    )

    def strip_at(t):
        main = lax.dynamic_slice_in_dim(field, t * STRIP, STRIP, 1)
        return [jnp.concatenate([main.reshape(nodes, GROUP), seam], 0)]

    halves = [strip_at(2 * (1 - h) + (x ^ flip))[0] for flip in range(2)]
    near = [lax.ppermute(halves[0], ALL, crossing(False, 0))]

    none = jnp.zeros((rows, GROUP), jnp.float32)
    pad = jnp.zeros((8 - rows, GROUP), jnp.float32)
    ends, between = [], []
    for t in (2, 3, 0, 1):
        left = field[:, t * STRIP - 1] if t > 0 else none
        right = field[:, (t + 1) * STRIP] if t < 3 else none
        main = field[:, t * STRIP : (t + 1) * STRIP]
        ends.append(jnp.concatenate([main[0], main[rows - 1], left, pad, right, pad], 0))
        between.append(main[1 : rows - 1].reshape((rows - 2) * STRIP, GROUP))
    ends = lax.all_to_all(jnp.stack(ends), PLACE, 0, 0, tiled=True)
    between = lax.all_to_all(jnp.stack(between), PLACE, 0, 0, tiled=True)
    half, ends = lax.optimization_barrier((halves[1], ends))
    near.append(lax.ppermute(half, ALL, crossing(False, 1)))

    total_nodes = snapshots.shape[0] * 4
    weight = weights_of(region_ids, conductivity) / math.sqrt(total_nodes)
    weight = jnp.pad(weight, ((0, 0), (8, 8)))
    weight = lax.dynamic_slice_in_dim(weight, (2 * (1 - l) + x) * STRIP, STRIP + 16, 1)
    weight = jnp.broadcast_to(weight[:, :, None], (rows, STRIP + 16, GROUP))

    def edge(at, r):
        return jnp.concatenate(
            [
                ends[:, at : at + STRIP],
                ends[:, 2 * STRIP + r : 2 * STRIP + r + 1],
                ends[:, 2 * STRIP + 8 + r : 2 * STRIP + 9 + r],
                jnp.zeros((4, 6, GROUP), jnp.float32),
            ],
            1,
        ).reshape(4 * (STRIP + 8), GROUP)

    above = jnp.concatenate([edge(STRIP, rows - 1), weight[rows - 1]], 0)
    below = edge(0, 0)
    above = lax.ppermute(above, TILE, [(m, m + 1) for m in range(3)])
    below = lax.ppermute(below, TILE, [(m + 1, m) for m in range(3)])
    half, near[0], below = lax.optimization_barrier((halves[0], near[0], below))
    far = [lax.ppermute(half, ALL, crossing(True, 0))]
    half, near[1], above, below = lax.optimization_barrier((halves[1], near[1], above, below))
    far.append(lax.ppermute(half, ALL, crossing(True, 1)))

    side = jnp.stack([c, h, x, l]).astype(jnp.int32)
    seam_side = jnp.stack([(h == 0) & (x == 1), (h == 1) & (x == 0)]).astype(jnp.float32)
    seam_side = seam_side * jnp.array([1.0, -1.0], jnp.float32)
    blocks = jax.ShapeDtypeStruct((8, GROUP, GROUP), jnp.float32)
    own_blocks = jax.ShapeDtypeStruct((2, 2, GROUP, 2 * GROUP), jnp.float32)
    half_float = jax.ShapeDtypeStruct((4 * GROUP, nodes + SEAM), jnp.bfloat16)
    high, low, own_mine, own_other = pl.pallas_call(
        lambda *refs: own_kernel(rows, *refs),
        out_shape=(half_float, half_float, own_blocks, own_blocks),
        in_specs=[SMEM] * 2 + [VMEM] * 5,
        out_specs=(VMEM,) * 4,
        scratch_shapes=[pltpu.VMEM((nodes, 4 * GROUP), jnp.bfloat16)] * 2
        + [pltpu.VMEM((nodes + SEAM, 4 * GROUP), jnp.bfloat16)] * 2,
        compiler_params=pltpu.CompilerParams(vmem_limit_bytes=40 * 1024 * 1024),
        cost_estimate=pl.CostEstimate(flops=1, bytes_accessed=1, transcendentals=0),
    )(side, seam_side, ends, between, above, below, weight)

    def both_cores(mine, other):
        return mine + lax.ppermute(other, "c", [(0, 1), (1, 0)])

    own = both_cores(own_mine, own_other)
    wide = [jax.ShapeDtypeStruct((4 * GROUP, n * GROUP), jnp.float32) for n in (2, 1)]
    early = pl.pallas_call(
        early_kernel,
        out_shape=wide,
        in_specs=[VMEM] * 5,
        out_specs=[VMEM] * 2,
        compiler_params=pltpu.CompilerParams(vmem_limit_bytes=40 * 1024 * 1024),
        cost_estimate=pl.CostEstimate(flops=1, bytes_accessed=1, transcendentals=0),
    )(high, low, *near, far[0])
    cross_mine, cross_other = pl.pallas_call(
        cross_kernel,
        out_shape=(blocks, blocks),
        in_specs=[SMEM] + [VMEM] * 5,
        out_specs=(VMEM,) * 2,
        scratch_shapes=[pltpu.VMEM((4 * GROUP, GROUP), jnp.float32)],
        compiler_params=pltpu.CompilerParams(vmem_limit_bytes=40 * 1024 * 1024),
        cost_estimate=pl.CostEstimate(flops=10**11, bytes_accessed=1, transcendentals=0),
    )(side, high, low, far[1], *early)

    cross = both_cores(cross_mine, cross_other)
    own, cross = lax.optimization_barrier((own, cross))
    own = own[0] + lax.ppermute(own[1], "l", [(0, 1), (1, 0)])
    own = own[0] + lax.ppermute(own[1], "x", [(0, 1), (1, 0)])
    to_holder = [
        (flat(i, j, k, 1 - i, n), flat(i, j, k, i, n))
        for i in range(2)
        for j in range(2)
        for k in range(2)
        for n in range(2)
    ]
    own = own + lax.ppermute(own, ALL, to_holder)

    cross = lax.all_to_all(cross, ALL, 0, 0, tiled=True, axis_index_groups=MIDDLE_GROUPS)
    cross = jnp.sum(cross, 0)
    even = (x + y) % 2 == 0
    turned = cross.T
    cross_pair = [
        lax.ppermute(jnp.where(even, cross, turned), ALL, owners(0)),
        lax.ppermute(jnp.where(even, turned, cross), ALL, owners(1)),
    ]
    swapped = (x + h) % 2 == 1
    left = jnp.where(swapped, cross_pair[1], cross_pair[0])
    right = jnp.where(swapped, cross_pair[0], cross_pair[1])
    return jnp.where(y == h, own, jnp.concatenate([left, right], 1))


def solution(mesh):
    sizes = (mesh.shape["snap"], mesh.shape["mesh"])

    def whole(snapshots, region_ids, conductivity):
        width = region_ids.shape[1]
        if sizes == (8, 4) and snapshots.shape[1] == 8 * GROUP and width == 4 * STRIP:
            parts = Mesh(mesh.devices.reshape(2, 2, 2, 2, 2), ALL)
            return jax.shard_map(
                local_strips,
                mesh=parts,
                in_specs=(P(TILE, ("h", "l", "x")), P(TILE, None), P()),
                out_specs=P(("h", "l", "x"), TILE),
                check_vma=False,
            )(snapshots, region_ids, conductivity)
        return jax.shard_map(
            local_ring,
            mesh=mesh,
            in_specs=(P("mesh", "snap"), P("mesh", None), P()),
            out_specs=P("snap", "mesh"),
            check_vma=False,
        )(snapshots, region_ids, conductivity)

    return whole
```

```python
import math

import jax
import jax.numpy as jnp
from jax import lax
from jax.experimental import pallas as pl
from jax.experimental.pallas import tpu as pltpu
from jax.sharding import Mesh
from jax.sharding import PartitionSpec as P


def passed_along(value, axis, steps):
    count = lax.axis_size(axis)
    first, last = (max(0, -steps), min(count, count - steps))
    return lax.ppermute(value, axis, [(source, source + steps) for source in range(first, last)])


def from_behind(block, axis, distance):
    devices = range(lax.axis_size(axis))
    route = [((i - distance) % len(devices), i) for i in devices]
    return lax.ppermute(block, axis, route)


def weights_of(region_ids, conductivity):
    table = jnp.arange(conductivity.shape[0], dtype=jnp.int32)
    picked = jnp.where(
        region_ids[:, :, None] == table[None, None, :],
        conductivity[None, None, :],
        jnp.zeros((), conductivity.dtype),
    )
    return jnp.sum(picked, axis=-1) / 36.0


def element_terms(field, below, weight):
    lower = jnp.concatenate([field, below[None]], 0)
    padded = jnp.pad(lower, ((0, 0), (0, 1), (0, 0)))
    corner_a = padded[:-1, :-1]
    corner_b = padded[:-1, 1:]
    corner_e = padded[1:, :-1]
    corner_d = padded[1:, 1:]
    scaled = weight[:, :, None]
    to_a = scaled * (4.0 * corner_a + 2.0 * corner_b + 2.0 * corner_e + corner_d)
    to_b = scaled * (2.0 * corner_a + 4.0 * corner_b + corner_e + 2.0 * corner_d)
    to_e = scaled * (2.0 * corner_a + corner_b + 4.0 * corner_e + 2.0 * corner_d)
    to_d = scaled * (corner_a + 2.0 * corner_b + 2.0 * corner_e + 4.0 * corner_d)
    total = jnp.pad(to_a, ((0, 1), (0, 1), (0, 0))) + jnp.pad(to_b, ((0, 1), (1, 0), (0, 0)))
    total = (
        total + jnp.pad(to_e, ((1, 0), (0, 1), (0, 0))) + jnp.pad(to_d, ((1, 0), (1, 0), (0, 0)))
    )
    return total


def contract(left, right):
    return lax.dot_general(
        left,
        right,
        (((0,), (0,)), ((), ())),
        precision=lax.Precision.HIGHEST,
        preferred_element_type=jnp.float32,
    )


def local_ring(snapshots, region_ids, conductivity):
    strip, width = region_ids.shape
    node_rows, group_cols = snapshots.shape
    field = snapshots.reshape(strip, width, group_cols)
    weight = weights_of(region_ids, conductivity)
    below = passed_along(field[0], "mesh", -1)
    total = element_terms(field, below, weight)
    carried = passed_along(total[strip, :width], "mesh", 1)
    inner = total[:strip, :width]
    panel = jnp.concatenate([inner[:1] + carried[None], inner[1:]], 0).reshape(
        node_rows, group_cols
    )
    count = lax.axis_size("snap")
    group = lax.axis_index("snap")
    reach = count // 2

    def place(partial_value, moving, step):
        tile = contract(snapshots, moving)
        source = (group - step) % count * group_cols
        return lax.dynamic_update_slice(partial_value, tile, (jnp.int32(0), source))

    partial_value = place(jnp.zeros((group_cols, group_cols * count), jnp.float32), panel, 0)

    def turn(step, carry):
        moving, partial_value = carry
        moving = from_behind(moving, "snap", 1)
        return (moving, place(partial_value, moving, step))

    _, partial_value = lax.fori_loop(1, reach + 1, turn, (panel, partial_value))
    blocks = jnp.transpose(partial_value.reshape(group_cols, count, group_cols), (1, 2, 0))
    target = jnp.arange(count, dtype=jnp.int32)
    offset = (group - target) % count
    valid = (offset >= 1) & (offset <= count - 1 - reach)
    outgoing = jnp.where(valid[:, None, None], blocks, jnp.zeros((), jnp.float32))
    incoming = lax.all_to_all(outgoing, "snap", split_axis=0, concat_axis=0, tiled=True)
    partial_value = partial_value + jnp.transpose(incoming, (1, 0, 2)).reshape(
        group_cols, count * group_cols
    )
    summed = lax.psum_scatter(partial_value, "mesh", scatter_dimension=1, tiled=True)
    total_nodes = node_rows * lax.axis_size("mesh")
    return summed / math.sqrt(total_nodes)


ALL = ("h", "l", "x", "y", "c")
PLACE = ("l", "x")
TILE = ("y", "c")
GROUP = 128
STRIP = 128
SEAM = 16


def flat(h, l, x, y, c):
    return (((h * 2 + l) * 2 + x) * 2 + y) * 2 + c


def crossing(outer, flip):
    pairs = []
    for h in range(2):
        l = h if outer else 1 - h
        for x in range(2):
            for y in range(2):
                for c in range(2):
                    pairs.append((flat(h, l, x, y, c), flat(1 - h, h, x ^ flip, y, c)))
    return pairs


def middle_groups():
    four = [(x, y) for x in range(2) for y in range(2)]
    groups = [[flat(h, 1 - h, x, y, c) for h in range(2) for x, y in four] for c in range(2)]
    groups += [[flat(h, h, x, y, c) for x, y in four for c in range(2)] for h in range(2)]
    return groups


def owners(turn):
    pairs = []
    for h in range(2):
        for x in range(2):
            for y in range(2):
                for c in range(2):
                    lower = flat(0, h, x, 1, c)
                    upper = flat(1, c, y, 0, h)
                    down = (x + y + turn) % 2 == 0
                    pairs.append((flat(h, 1 - h, x, y, c), lower if down else upper))
    return pairs


MIDDLE_GROUPS = middle_groups()


def split(value):
    high = value.astype(jnp.bfloat16)
    return high, (value - high.astype(jnp.float32)).astype(jnp.bfloat16)


def product(left_high, left_low, right_high, right_low, turned=False):
    def one(a, b):
        return lax.dot_general(
            a, b, (((1 if turned else 0,), (0,)), ((), ())), preferred_element_type=jnp.float32
        )

    return one(left_high, right_high) + one(left_high, right_low) + one(left_low, right_high)


def own_kernel(
    rows,
    side_ref,
    seam_ref,
    ends_ref,
    field_ref,
    above_ref,
    below_ref,
    weight_ref,
    high_ref,
    low_ref,
    mine_ref,
    other_ref,
    sh,
    sl,
    ph,
    pw,
):
    wide = STRIP + 16
    line_number = lax.broadcasted_iota(jnp.int32, (SEAM, GROUP), 0)
    first_core = side_ref[0] == 0
    x, l = side_ref[2], side_ref[3]

    def line(main, left, right):
        return jnp.concatenate(
            [
                jnp.broadcast_to(left, (8, GROUP)),
                main,
                jnp.broadcast_to(right, (8, GROUP)),
            ],
            0,
        )

    def halo(ref, g):
        at = g * (STRIP + 8)
        end = at + STRIP
        return line(ref[at:end], ref[end : end + 1], ref[end + 1 : end + 2])

    body = rows * STRIP
    for g in range(4):
        columns = slice(g * GROUP, (g + 1) * GROUP)
        before = halo(above_ref, g)
        before_up = pltpu.roll(before, wide - 1, 0)
        carried = carried_next = None
        seam = jnp.zeros((SEAM, GROUP), jnp.float32)
        for r in range(-1, rows):
            n = r + 1
            if n < rows:
                if n in (0, rows - 1):
                    at = 0 if n == 0 else STRIP
                    main = ends_ref[g, at : at + STRIP]
                else:
                    main = field_ref[g, (n - 1) * STRIP : n * STRIP]
                sides = 2 * STRIP + n
                after = line(
                    main,
                    ends_ref[g, sides : sides + 1],
                    ends_ref[g, sides + 8 : sides + 9],
                )
                high, low = split(main)
                sh[n * STRIP : (n + 1) * STRIP, columns] = high
                sl[n * STRIP : (n + 1) * STRIP, columns] = low
            else:
                after = halo(below_ref, g)
            after_up = pltpu.roll(after, wide - 1, 0)
            weight = weight_ref[r] if r >= 0 else above_ref[4 * (STRIP + 8) :]
            top, top_up = 2.0 * before + after, 2.0 * before_up + after_up
            to_a, to_b = weight * (2.0 * top + top_up), weight * (top + 2.0 * top_up)
            if r >= 0:
                from_left = pltpu.roll(to_b + carried_next, 1, 0)
                total = to_a + carried + from_left
                beside = (
                    seam_ref[0] * from_left[8 + STRIP : 9 + STRIP] + seam_ref[1] * from_left[8:9]
                )
                seam = jnp.where(line_number == r, beside, seam)
                high, low = split(total[8 : 8 + STRIP])
                ph[r * STRIP : (r + 1) * STRIP, columns] = high
                pw[r * STRIP : (r + 1) * STRIP, columns] = low
            low_end, low_up = before + 2.0 * after, before_up + 2.0 * after_up
            carried = weight * (2.0 * low_end + low_up)
            carried_next = weight * (low_end + 2.0 * low_up)
            before, before_up = after, after_up
        high, low = split(seam)
        ph[body : body + SEAM, columns] = high
        pw[body : body + SEAM, columns] = low
    for a in range(2):
        left = slice(a * 256, (a + 1) * 256)
        tiles = [
            product(
                sh[:, left], sl[:, left], ph[:body, right], pw[:body, right]
            )
            for right in (slice(0, 256), slice(256, 512))
        ]
        mine = jnp.where(first_core, tiles[0], tiles[1])
        other = jnp.where(first_core, tiles[1], tiles[0])
        for i in range(2):
            rows_of = slice(i * GROUP, (i + 1) * GROUP)
            mine_ref[l ^ a, x ^ i] = mine[rows_of]
            other_ref[l ^ a, x ^ i] = other[rows_of]
    for turned_ref, panel in ((high_ref, ph), (low_ref, pw)):
        turned_ref[...] = panel[...].T


def early_kernel(high_ref, low_ref, s0, s1, s2, pair_ref, third_ref):
    h0, l0 = split(s0[...])
    h1, l1 = split(s1[...])
    sh = jnp.concatenate([h0, h1], 1)
    sl = jnp.concatenate([l0, l1], 1)
    pair_ref[...] = product(high_ref[...], low_ref[...], sh, sl, turned=True)
    sh, sl = split(s2[...])
    third_ref[...] = product(high_ref[...], low_ref[...], sh, sl, turned=True)


def cross_kernel(side_ref, high_ref, low_ref, last, pair_ref, third_ref, mine_ref, other_ref, fourth):
    core, half, x = side_ref[0], side_ref[1], side_ref[2]
    sh, sl = split(last[...])
    fourth[...] = product(high_ref[...], low_ref[...], sh, sl, turned=True)

    def place(h, c):
        for pair in range(2):
            for a in range(2):
                ref = mine_ref if (a if h else pair) == c else other_ref
                for i in range(2):
                    for j in range(2):
                        rows_of = slice((2 * a + i) * GROUP, (2 * a + i + 1) * GROUP)
                        if pair == 0:
                            block = pair_ref[rows_of, j * GROUP : (j + 1) * GROUP]
                        else:
                            block = (fourth if j else third_ref)[rows_of]
                        if h:
                            ref[(2 * (1 - pair) + (x ^ j)) * 2 + i] = block.T
                        else:
                            ref[(2 * a + i) * 2 + (x ^ j)] = block

    for h in range(2):
        for c in range(2):
            pl.when((half == h) & (core == c))(lambda: place(h, c))


VMEM = pl.BlockSpec(memory_space=pltpu.VMEM)
SMEM = pl.BlockSpec(memory_space=pltpu.SMEM)


def local_strips(snapshots, region_ids, conductivity):
    rows, width = region_ids.shape
    nodes = rows * STRIP
    field = snapshots.reshape(rows, width, GROUP)
    h, l, x, y, c = (lax.axis_index(a) for a in ALL)

    seam = jnp.concatenate(
        [field[:, 2 * STRIP], jnp.zeros((SEAM - rows, GROUP), jnp.float32)], 0
    )

    def strip_at(t):
        main = lax.dynamic_slice_in_dim(field, t * STRIP, STRIP, 1)
        return [jnp.concatenate([main.reshape(nodes, GROUP), seam], 0)]

    halves = [strip_at(2 * (1 - h) + (x ^ flip))[0] for flip in range(2)]
    near = [lax.ppermute(halves[0], ALL, crossing(False, 0))]

    none = jnp.zeros((rows, GROUP), jnp.float32)
    pad = jnp.zeros((8 - rows, GROUP), jnp.float32)
    ends, between = [], []
    for t in (2, 3, 0, 1):
        left = field[:, t * STRIP - 1] if t > 0 else none
        right = field[:, (t + 1) * STRIP] if t < 3 else none
        main = field[:, t * STRIP : (t + 1) * STRIP]
        ends.append(jnp.concatenate([main[0], main[rows - 1], left, pad, right, pad], 0))
        between.append(main[1 : rows - 1].reshape((rows - 2) * STRIP, GROUP))
    ends = lax.all_to_all(jnp.stack(ends), PLACE, 0, 0, tiled=True)
    between = lax.all_to_all(jnp.stack(between), PLACE, 0, 0, tiled=True)
    half, ends = lax.optimization_barrier((halves[1], ends))
    near.append(lax.ppermute(half, ALL, crossing(False, 1)))

    total_nodes = snapshots.shape[0] * 4
    weight = weights_of(region_ids, conductivity) / math.sqrt(total_nodes)
    weight = jnp.pad(weight, ((0, 0), (8, 8)))
    weight = lax.dynamic_slice_in_dim(weight, (2 * (1 - l) + x) * STRIP, STRIP + 16, 1)
    weight = jnp.broadcast_to(weight[:, :, None], (rows, STRIP + 16, GROUP))

    def edge(at, r):
        return jnp.concatenate(
            [
                ends[:, at : at + STRIP],
                ends[:, 2 * STRIP + r : 2 * STRIP + r + 1],
                ends[:, 2 * STRIP + 8 + r : 2 * STRIP + 9 + r],
                jnp.zeros((4, 6, GROUP), jnp.float32),
            ],
            1,
        ).reshape(4 * (STRIP + 8), GROUP)

    above = jnp.concatenate([edge(STRIP, rows - 1), weight[rows - 1]], 0)
    below = edge(0, 0)
    above = lax.ppermute(above, TILE, [(m, m + 1) for m in range(3)])
    below = lax.ppermute(below, TILE, [(m + 1, m) for m in range(3)])
    half, near[0], below = lax.optimization_barrier((halves[0], near[0], below))
    far = [lax.ppermute(half, ALL, crossing(True, 0))]
    half, near[1], above, below = lax.optimization_barrier((halves[1], near[1], above, below))
    far.append(lax.ppermute(half, ALL, crossing(True, 1)))

    side = jnp.stack([c, h, x, l]).astype(jnp.int32)
    seam_side = jnp.stack([(h == 0) & (x == 1), (h == 1) & (x == 0)]).astype(jnp.float32)
    seam_side = seam_side * jnp.array([1.0, -1.0], jnp.float32)
    blocks = jax.ShapeDtypeStruct((8, GROUP, GROUP), jnp.float32)
    own_blocks = jax.ShapeDtypeStruct((2, 2, GROUP, 2 * GROUP), jnp.float32)
    half_float = jax.ShapeDtypeStruct((4 * GROUP, nodes + SEAM), jnp.bfloat16)
    high, low, own_mine, own_other = pl.pallas_call(
        lambda *refs: own_kernel(rows, *refs),
        out_shape=(half_float, half_float, own_blocks, own_blocks),
        in_specs=[SMEM] * 2 + [VMEM] * 5,
        out_specs=(VMEM,) * 4,
        scratch_shapes=[pltpu.VMEM((nodes, 4 * GROUP), jnp.bfloat16)] * 2
        + [pltpu.VMEM((nodes + SEAM, 4 * GROUP), jnp.bfloat16)] * 2,
        compiler_params=pltpu.CompilerParams(vmem_limit_bytes=40 * 1024 * 1024),
        cost_estimate=pl.CostEstimate(flops=1, bytes_accessed=1, transcendentals=0),
    )(side, seam_side, ends, between, above, below, weight)

    def both_cores(mine, other):
        return mine + lax.ppermute(other, "c", [(0, 1), (1, 0)])

    own = both_cores(own_mine, own_other)
    wide = [jax.ShapeDtypeStruct((4 * GROUP, n * GROUP), jnp.float32) for n in (2, 1)]
    early = pl.pallas_call(
        early_kernel,
        out_shape=wide,
        in_specs=[VMEM] * 5,
        out_specs=[VMEM] * 2,
        compiler_params=pltpu.CompilerParams(vmem_limit_bytes=40 * 1024 * 1024),
        cost_estimate=pl.CostEstimate(flops=1, bytes_accessed=1, transcendentals=0),
    )(high, low, *near, far[0])
    cross_mine, cross_other = pl.pallas_call(
        cross_kernel,
        out_shape=(blocks, blocks),
        in_specs=[SMEM] + [VMEM] * 5,
        out_specs=(VMEM,) * 2,
        scratch_shapes=[pltpu.VMEM((4 * GROUP, GROUP), jnp.float32)],
        compiler_params=pltpu.CompilerParams(vmem_limit_bytes=40 * 1024 * 1024),
        cost_estimate=pl.CostEstimate(flops=1, bytes_accessed=1, transcendentals=0),
    )(side, high, low, far[1], *early)

    cross = both_cores(cross_mine, cross_other)
    own, cross = lax.optimization_barrier((own, cross))
    own = own[0] + lax.ppermute(own[1], "l", [(0, 1), (1, 0)])
    own = own[0] + lax.ppermute(own[1], "x", [(0, 1), (1, 0)])
    to_holder = [
        (flat(i, j, k, 1 - i, n), flat(i, j, k, i, n))
        for i in range(2)
        for j in range(2)
        for k in range(2)
        for n in range(2)
    ]
    own = own + lax.ppermute(own, ALL, to_holder)

    cross = lax.all_to_all(cross, ALL, 0, 0, tiled=True, axis_index_groups=MIDDLE_GROUPS)
    cross = jnp.sum(cross, 0)
    even = (x + y) % 2 == 0
    turned = cross.T
    cross_pair = [
        lax.ppermute(jnp.where(even, cross, turned), ALL, owners(0)),
        lax.ppermute(jnp.where(even, turned, cross), ALL, owners(1)),
    ]
    swapped = (x + h) % 2 == 1
    left = jnp.where(swapped, cross_pair[1], cross_pair[0])
    right = jnp.where(swapped, cross_pair[0], cross_pair[1])
    return jnp.where(y == h, own, jnp.concatenate([left, right], 1))


def solution(mesh):
    sizes = (mesh.shape["snap"], mesh.shape["mesh"])

    def whole(snapshots, region_ids, conductivity):
        width = region_ids.shape[1]
        if sizes == (8, 4) and snapshots.shape[1] == 8 * GROUP and width == 4 * STRIP:
            parts = Mesh(mesh.devices.reshape(2, 2, 2, 2, 2), ALL)
            return jax.shard_map(
                local_strips,
                mesh=parts,
                in_specs=(P(TILE, ("h", "l", "x")), P(TILE, None), P()),
                out_specs=P(("h", "l", "x"), TILE),
                check_vma=False,
            )(snapshots, region_ids, conductivity)
        return jax.shard_map(
            local_ring,
            mesh=mesh,
            in_specs=(P("mesh", "snap"), P("mesh", None), P()),
            out_specs=P("snap", "mesh"),
            check_vma=False,
        )(snapshots, region_ids, conductivity)

    return whole
```

```python
import math

import jax
import jax.numpy as jnp
from jax import lax
from jax.experimental import pallas as pl
from jax.experimental.pallas import tpu as pltpu
from jax.sharding import Mesh
from jax.sharding import PartitionSpec as P


def passed_along(value, axis, steps):
    count = lax.axis_size(axis)
    first, last = (max(0, -steps), min(count, count - steps))
    return lax.ppermute(value, axis, [(source, source + steps) for source in range(first, last)])


def from_behind(block, axis, distance):
    devices = range(lax.axis_size(axis))
    route = [((i - distance) % len(devices), i) for i in devices]
    return lax.ppermute(block, axis, route)


def weights_of(region_ids, conductivity):
    table = jnp.arange(conductivity.shape[0], dtype=jnp.int32)
    picked = jnp.where(
        region_ids[:, :, None] == table[None, None, :],
        conductivity[None, None, :],
        jnp.zeros((), conductivity.dtype),
    )
    return jnp.sum(picked, axis=-1) / 36.0


def element_terms(field, below, weight):
    lower = jnp.concatenate([field, below[None]], 0)
    padded = jnp.pad(lower, ((0, 0), (0, 1), (0, 0)))
    corner_a = padded[:-1, :-1]
    corner_b = padded[:-1, 1:]
    corner_e = padded[1:, :-1]
    corner_d = padded[1:, 1:]
    scaled = weight[:, :, None]
    to_a = scaled * (4.0 * corner_a + 2.0 * corner_b + 2.0 * corner_e + corner_d)
    to_b = scaled * (2.0 * corner_a + 4.0 * corner_b + corner_e + 2.0 * corner_d)
    to_e = scaled * (2.0 * corner_a + corner_b + 4.0 * corner_e + 2.0 * corner_d)
    to_d = scaled * (corner_a + 2.0 * corner_b + 2.0 * corner_e + 4.0 * corner_d)
    total = jnp.pad(to_a, ((0, 1), (0, 1), (0, 0))) + jnp.pad(to_b, ((0, 1), (1, 0), (0, 0)))
    total = (
        total + jnp.pad(to_e, ((1, 0), (0, 1), (0, 0))) + jnp.pad(to_d, ((1, 0), (1, 0), (0, 0)))
    )
    return total


def contract(left, right):
    return lax.dot_general(
        left,
        right,
        (((0,), (0,)), ((), ())),
        precision=lax.Precision.HIGHEST,
        preferred_element_type=jnp.float32,
    )


def local_ring(snapshots, region_ids, conductivity):
    strip, width = region_ids.shape
    node_rows, group_cols = snapshots.shape
    field = snapshots.reshape(strip, width, group_cols)
    weight = weights_of(region_ids, conductivity)
    below = passed_along(field[0], "mesh", -1)
    total = element_terms(field, below, weight)
    carried = passed_along(total[strip, :width], "mesh", 1)
    inner = total[:strip, :width]
    panel = jnp.concatenate([inner[:1] + carried[None], inner[1:]], 0).reshape(
        node_rows, group_cols
    )
    count = lax.axis_size("snap")
    group = lax.axis_index("snap")
    reach = count // 2

    def place(partial_value, moving, step):
        tile = contract(snapshots, moving)
        source = (group - step) % count * group_cols
        return lax.dynamic_update_slice(partial_value, tile, (jnp.int32(0), source))

    partial_value = place(jnp.zeros((group_cols, group_cols * count), jnp.float32), panel, 0)

    def turn(step, carry):
        moving, partial_value = carry
        moving = from_behind(moving, "snap", 1)
        return (moving, place(partial_value, moving, step))

    _, partial_value = lax.fori_loop(1, reach + 1, turn, (panel, partial_value))
    blocks = jnp.transpose(partial_value.reshape(group_cols, count, group_cols), (1, 2, 0))
    target = jnp.arange(count, dtype=jnp.int32)
    offset = (group - target) % count
    valid = (offset >= 1) & (offset <= count - 1 - reach)
    outgoing = jnp.where(valid[:, None, None], blocks, jnp.zeros((), jnp.float32))
    incoming = lax.all_to_all(outgoing, "snap", split_axis=0, concat_axis=0, tiled=True)
    partial_value = partial_value + jnp.transpose(incoming, (1, 0, 2)).reshape(
        group_cols, count * group_cols
    )
    summed = lax.psum_scatter(partial_value, "mesh", scatter_dimension=1, tiled=True)
    total_nodes = node_rows * lax.axis_size("mesh")
    return summed / math.sqrt(total_nodes)


ALL = ("h", "l", "x", "y", "c")
PLACE = ("l", "x")
TILE = ("y", "c")
GROUP = 128
STRIP = 128
SEAM = 16


def flat(h, l, x, y, c):
    return (((h * 2 + l) * 2 + x) * 2 + y) * 2 + c


def crossing(outer, flip):
    pairs = []
    for h in range(2):
        l = h if outer else 1 - h
        for x in range(2):
            for y in range(2):
                for c in range(2):
                    pairs.append((flat(h, l, x, y, c), flat(1 - h, h, x ^ flip, y, c)))
    return pairs


def middle_groups():
    four = [(x, y) for x in range(2) for y in range(2)]
    groups = [[flat(h, 1 - h, x, y, c) for h in range(2) for x, y in four] for c in range(2)]
    groups += [[flat(h, h, x, y, c) for x, y in four for c in range(2)] for h in range(2)]
    return groups


def owners(turn):
    pairs = []
    for h in range(2):
        for x in range(2):
            for y in range(2):
                for c in range(2):
                    lower = flat(0, h, x, 1, c)
                    upper = flat(1, c, y, 0, h)
                    down = (x + y + turn) % 2 == 0
                    pairs.append((flat(h, 1 - h, x, y, c), lower if down else upper))
    return pairs


MIDDLE_GROUPS = middle_groups()


def split(value):
    high = value.astype(jnp.bfloat16)
    return high, (value - high.astype(jnp.float32)).astype(jnp.bfloat16)


def product(left_high, left_low, right_high, right_low, turned=False):
    def one(a, b):
        return lax.dot_general(
            a, b, (((1 if turned else 0,), (0,)), ((), ())), preferred_element_type=jnp.float32
        )

    return one(left_high, right_high) + one(left_high, right_low) + one(left_low, right_high)


def own_kernel(
    rows,
    side_ref,
    seam_ref,
    ends_ref,
    field_ref,
    above_ref,
    below_ref,
    weight_ref,
    high_ref,
    low_ref,
    mine_ref,
    other_ref,
    sh,
    sl,
    ph,
    pw,
):
    wide = STRIP + 16
    line_number = lax.broadcasted_iota(jnp.int32, (SEAM, GROUP), 0)
    first_core = side_ref[0] == 0
    x, l = side_ref[2], side_ref[3]

    def line(main, left, right):
        return jnp.concatenate(
            [
                jnp.broadcast_to(left, (8, GROUP)),
                main,
                jnp.broadcast_to(right, (8, GROUP)),
            ],
            0,
        )

    def halo(ref, g):
        at = g * (STRIP + 8)
        end = at + STRIP
        return line(ref[at:end], ref[end : end + 1], ref[end + 1 : end + 2])

    body = rows * STRIP
    for g in range(4):
        columns = slice(g * GROUP, (g + 1) * GROUP)
        before = halo(above_ref, g)
        before_up = pltpu.roll(before, wide - 1, 0)
        carried = carried_next = None
        seam = jnp.zeros((SEAM, GROUP), jnp.float32)
        for r in range(-1, rows):
            n = r + 1
            if n < rows:
                if n in (0, rows - 1):
                    at = 0 if n == 0 else STRIP
                    main = ends_ref[g, at : at + STRIP]
                else:
                    main = field_ref[g, (n - 1) * STRIP : n * STRIP]
                sides = 2 * STRIP + n
                after = line(
                    main,
                    ends_ref[g, sides : sides + 1],
                    ends_ref[g, sides + 8 : sides + 9],
                )
                high, low = split(main)
                sh[n * STRIP : (n + 1) * STRIP, columns] = high
                sl[n * STRIP : (n + 1) * STRIP, columns] = low
            else:
                after = halo(below_ref, g)
            after_up = pltpu.roll(after, wide - 1, 0)
            weight = weight_ref[r] if r >= 0 else above_ref[4 * (STRIP + 8) :]
            top, top_up = 2.0 * before + after, 2.0 * before_up + after_up
            to_a, to_b = weight * (2.0 * top + top_up), weight * (top + 2.0 * top_up)
            if r >= 0:
                from_left = pltpu.roll(to_b + carried_next, 1, 0)
                total = to_a + carried + from_left
                beside = (
                    seam_ref[0] * from_left[8 + STRIP : 9 + STRIP] + seam_ref[1] * from_left[8:9]
                )
                seam = jnp.where(line_number == r, beside, seam)
                high, low = split(total[8 : 8 + STRIP])
                ph[r * STRIP : (r + 1) * STRIP, columns] = high
                pw[r * STRIP : (r + 1) * STRIP, columns] = low
            low_end, low_up = before + 2.0 * after, before_up + 2.0 * after_up
            carried = weight * (2.0 * low_end + low_up)
            carried_next = weight * (low_end + 2.0 * low_up)
            before, before_up = after, after_up
        high, low = split(seam)
        ph[body : body + SEAM, columns] = high
        pw[body : body + SEAM, columns] = low
    for a in range(2):
        left = slice(a * 256, (a + 1) * 256)
        tiles = [
            product(
                sh[:, left], sl[:, left], ph[:body, right], pw[:body, right]
            )
            for right in (slice(0, 256), slice(256, 512))
        ]
        mine = jnp.where(first_core, tiles[0], tiles[1])
        other = jnp.where(first_core, tiles[1], tiles[0])
        for i in range(2):
            rows_of = slice(i * GROUP, (i + 1) * GROUP)
            mine_ref[l ^ a, x ^ i] = mine[rows_of]
            other_ref[l ^ a, x ^ i] = other[rows_of]
    for turned_ref, panel in ((high_ref, ph), (low_ref, pw)):
        turned_ref[...] = panel[...].T


def early_kernel(high_ref, low_ref, s0, s1, s2, pair_ref, third_ref):
    h0, l0 = split(s0[...])
    h1, l1 = split(s1[...])
    sh = jnp.concatenate([h0, h1], 1)
    sl = jnp.concatenate([l0, l1], 1)
    pair_ref[...] = product(high_ref[...], low_ref[...], sh, sl, turned=True)
    sh, sl = split(s2[...])
    third_ref[...] = product(high_ref[...], low_ref[...], sh, sl, turned=True)


def cross_kernel(side_ref, high_ref, low_ref, last, pair_ref, third_ref, mine_ref, other_ref, fourth):
    core, half, x = side_ref[0], side_ref[1], side_ref[2]
    sh, sl = split(last[...])
    fourth[...] = product(high_ref[...], low_ref[...], sh, sl, turned=True)

    def place(h, c):
        for pair in range(2):
            for a in range(2):
                ref = mine_ref if (a if h else pair) == c else other_ref
                for i in range(2):
                    for j in range(2):
                        rows_of = slice((2 * a + i) * GROUP, (2 * a + i + 1) * GROUP)
                        if pair == 0:
                            block = pair_ref[rows_of, j * GROUP : (j + 1) * GROUP]
                        else:
                            block = (third_ref if j else fourth)[rows_of]
                        if h:
                            ref[(2 * (1 - pair) + (x ^ j)) * 2 + i] = block.T
                        else:
                            ref[(2 * a + i) * 2 + (x ^ j)] = block

    for h in range(2):
        for c in range(2):
            pl.when((half == h) & (core == c))(lambda: place(h, c))


VMEM = pl.BlockSpec(memory_space=pltpu.VMEM)
SMEM = pl.BlockSpec(memory_space=pltpu.SMEM)


def local_strips(snapshots, region_ids, conductivity):
    rows, width = region_ids.shape
    nodes = rows * STRIP
    field = snapshots.reshape(rows, width, GROUP)
    h, l, x, y, c = (lax.axis_index(a) for a in ALL)

    seam = jnp.concatenate(
        [field[:, 2 * STRIP], jnp.zeros((SEAM - rows, GROUP), jnp.float32)], 0
    )

    def strip_at(t):
        main = lax.dynamic_slice_in_dim(field, t * STRIP, STRIP, 1)
        return [jnp.concatenate([main.reshape(nodes, GROUP), seam], 0)]

    halves = [strip_at(2 * (1 - h) + (x ^ flip))[0] for flip in range(2)]
    near = [lax.ppermute(halves[0], ALL, crossing(False, 0))]

    none = jnp.zeros((rows, GROUP), jnp.float32)
    pad = jnp.zeros((8 - rows, GROUP), jnp.float32)
    ends, between = [], []
    for t in (2, 3, 0, 1):
        left = field[:, t * STRIP - 1] if t > 0 else none
        right = field[:, (t + 1) * STRIP] if t < 3 else none
        main = field[:, t * STRIP : (t + 1) * STRIP]
        ends.append(jnp.concatenate([main[0], main[rows - 1], left, pad, right, pad], 0))
        between.append(main[1 : rows - 1].reshape((rows - 2) * STRIP, GROUP))
    ends = lax.all_to_all(jnp.stack(ends), PLACE, 0, 0, tiled=True)
    between = lax.all_to_all(jnp.stack(between), PLACE, 0, 0, tiled=True)
    half, ends = lax.optimization_barrier((halves[1], ends))
    near.append(lax.ppermute(half, ALL, crossing(False, 1)))

    total_nodes = snapshots.shape[0] * 4
    weight = weights_of(region_ids, conductivity) / math.sqrt(total_nodes)
    weight = jnp.pad(weight, ((0, 0), (8, 8)))
    weight = lax.dynamic_slice_in_dim(weight, (2 * (1 - l) + x) * STRIP, STRIP + 16, 1)
    weight = jnp.broadcast_to(weight[:, :, None], (rows, STRIP + 16, GROUP))

    def edge(at, r):
        return jnp.concatenate(
            [
                ends[:, at : at + STRIP],
                ends[:, 2 * STRIP + r : 2 * STRIP + r + 1],
                ends[:, 2 * STRIP + 8 + r : 2 * STRIP + 9 + r],
                jnp.zeros((4, 6, GROUP), jnp.float32),
            ],
            1,
        ).reshape(4 * (STRIP + 8), GROUP)

    above = jnp.concatenate([edge(STRIP, rows - 1), weight[rows - 1]], 0)
    below = edge(0, 0)
    above = lax.ppermute(above, TILE, [(m, m + 1) for m in range(3)])
    below = lax.ppermute(below, TILE, [(m + 1, m) for m in range(3)])
    half, near[0], below = lax.optimization_barrier((halves[1], near[0], below))
    far = [lax.ppermute(half, ALL, crossing(True, 1))]
    half, near[1], above, below = lax.optimization_barrier((halves[0], near[1], above, below))
    far.append(lax.ppermute(half, ALL, crossing(True, 0)))

    side = jnp.stack([c, h, x, l]).astype(jnp.int32)
    seam_side = jnp.stack([(h == 0) & (x == 1), (h == 1) & (x == 0)]).astype(jnp.float32)
    seam_side = seam_side * jnp.array([1.0, -1.0], jnp.float32)
    blocks = jax.ShapeDtypeStruct((8, GROUP, GROUP), jnp.float32)
    own_blocks = jax.ShapeDtypeStruct((2, 2, GROUP, 2 * GROUP), jnp.float32)
    half_float = jax.ShapeDtypeStruct((4 * GROUP, nodes + SEAM), jnp.bfloat16)
    high, low, own_mine, own_other = pl.pallas_call(
        lambda *refs: own_kernel(rows, *refs),
        out_shape=(half_float, half_float, own_blocks, own_blocks),
        in_specs=[SMEM] * 2 + [VMEM] * 5,
        out_specs=(VMEM,) * 4,
        scratch_shapes=[pltpu.VMEM((nodes, 4 * GROUP), jnp.bfloat16)] * 2
        + [pltpu.VMEM((nodes + SEAM, 4 * GROUP), jnp.bfloat16)] * 2,
        compiler_params=pltpu.CompilerParams(vmem_limit_bytes=40 * 1024 * 1024),
        cost_estimate=pl.CostEstimate(flops=1, bytes_accessed=1, transcendentals=0),
    )(side, seam_side, ends, between, above, below, weight)

    def both_cores(mine, other):
        return mine + lax.ppermute(other, "c", [(0, 1), (1, 0)])

    own = both_cores(own_mine, own_other)
    wide = [jax.ShapeDtypeStruct((4 * GROUP, n * GROUP), jnp.float32) for n in (2, 1)]
    early = pl.pallas_call(
        early_kernel,
        out_shape=wide,
        in_specs=[VMEM] * 5,
        out_specs=[VMEM] * 2,
        compiler_params=pltpu.CompilerParams(vmem_limit_bytes=40 * 1024 * 1024),
        cost_estimate=pl.CostEstimate(flops=1, bytes_accessed=1, transcendentals=0),
    )(high, low, *near, far[0])
    cross_mine, cross_other = pl.pallas_call(
        cross_kernel,
        out_shape=(blocks, blocks),
        in_specs=[SMEM] + [VMEM] * 5,
        out_specs=(VMEM,) * 2,
        scratch_shapes=[pltpu.VMEM((4 * GROUP, GROUP), jnp.float32)],
        compiler_params=pltpu.CompilerParams(vmem_limit_bytes=40 * 1024 * 1024),
        cost_estimate=pl.CostEstimate(flops=1, bytes_accessed=1, transcendentals=0),
    )(side, high, low, far[1], *early)

    cross = both_cores(cross_mine, cross_other)
    own, cross = lax.optimization_barrier((own, cross))
    own = own[0] + lax.ppermute(own[1], "l", [(0, 1), (1, 0)])
    own = own[0] + lax.ppermute(own[1], "x", [(0, 1), (1, 0)])
    to_holder = [
        (flat(i, j, k, 1 - i, n), flat(i, j, k, i, n))
        for i in range(2)
        for j in range(2)
        for k in range(2)
        for n in range(2)
    ]
    own = own + lax.ppermute(own, ALL, to_holder)

    cross = lax.all_to_all(cross, ALL, 0, 0, tiled=True, axis_index_groups=MIDDLE_GROUPS)
    cross = jnp.sum(cross, 0)
    even = (x + y) % 2 == 0
    turned = cross.T
    cross_pair = [
        lax.ppermute(jnp.where(even, cross, turned), ALL, owners(0)),
        lax.ppermute(jnp.where(even, turned, cross), ALL, owners(1)),
    ]
    swapped = (x + h) % 2 == 1
    left = jnp.where(swapped, cross_pair[1], cross_pair[0])
    right = jnp.where(swapped, cross_pair[0], cross_pair[1])
    return jnp.where(y == h, own, jnp.concatenate([left, right], 1))


def solution(mesh):
    sizes = (mesh.shape["snap"], mesh.shape["mesh"])

    def whole(snapshots, region_ids, conductivity):
        width = region_ids.shape[1]
        if sizes == (8, 4) and snapshots.shape[1] == 8 * GROUP and width == 4 * STRIP:
            parts = Mesh(mesh.devices.reshape(2, 2, 2, 2, 2), ALL)
            return jax.shard_map(
                local_strips,
                mesh=parts,
                in_specs=(P(TILE, ("h", "l", "x")), P(TILE, None), P()),
                out_specs=P(("h", "l", "x"), TILE),
                check_vma=False,
            )(snapshots, region_ids, conductivity)
        return jax.shard_map(
            local_ring,
            mesh=mesh,
            in_specs=(P("mesh", "snap"), P("mesh", None), P()),
            out_specs=P("snap", "mesh"),
            check_vma=False,
        )(snapshots, region_ids, conductivity)

    return whole
```

```python
import math

import jax
import jax.numpy as jnp
from jax import lax
from jax.experimental import pallas as pl
from jax.experimental.pallas import tpu as pltpu
from jax.sharding import Mesh
from jax.sharding import PartitionSpec as P


def passed_along(value, axis, steps):
    count = lax.axis_size(axis)
    first, last = (max(0, -steps), min(count, count - steps))
    return lax.ppermute(value, axis, [(source, source + steps) for source in range(first, last)])


def from_behind(block, axis, distance):
    devices = range(lax.axis_size(axis))
    route = [((i - distance) % len(devices), i) for i in devices]
    return lax.ppermute(block, axis, route)


def weights_of(region_ids, conductivity):
    table = jnp.arange(conductivity.shape[0], dtype=jnp.int32)
    picked = jnp.where(
        region_ids[:, :, None] == table[None, None, :],
        conductivity[None, None, :],
        jnp.zeros((), conductivity.dtype),
    )
    return jnp.sum(picked, axis=-1) / 36.0


def element_terms(field, below, weight):
    lower = jnp.concatenate([field, below[None]], 0)
    padded = jnp.pad(lower, ((0, 0), (0, 1), (0, 0)))
    corner_a = padded[:-1, :-1]
    corner_b = padded[:-1, 1:]
    corner_e = padded[1:, :-1]
    corner_d = padded[1:, 1:]
    scaled = weight[:, :, None]
    to_a = scaled * (4.0 * corner_a + 2.0 * corner_b + 2.0 * corner_e + corner_d)
    to_b = scaled * (2.0 * corner_a + 4.0 * corner_b + corner_e + 2.0 * corner_d)
    to_e = scaled * (2.0 * corner_a + corner_b + 4.0 * corner_e + 2.0 * corner_d)
    to_d = scaled * (corner_a + 2.0 * corner_b + 2.0 * corner_e + 4.0 * corner_d)
    total = jnp.pad(to_a, ((0, 1), (0, 1), (0, 0))) + jnp.pad(to_b, ((0, 1), (1, 0), (0, 0)))
    total = (
        total + jnp.pad(to_e, ((1, 0), (0, 1), (0, 0))) + jnp.pad(to_d, ((1, 0), (1, 0), (0, 0)))
    )
    return total


def contract(left, right):
    return lax.dot_general(
        left,
        right,
        (((0,), (0,)), ((), ())),
        precision=lax.Precision.HIGHEST,
        preferred_element_type=jnp.float32,
    )


def local_ring(snapshots, region_ids, conductivity):
    strip, width = region_ids.shape
    node_rows, group_cols = snapshots.shape
    field = snapshots.reshape(strip, width, group_cols)
    weight = weights_of(region_ids, conductivity)
    below = passed_along(field[0], "mesh", -1)
    total = element_terms(field, below, weight)
    carried = passed_along(total[strip, :width], "mesh", 1)
    inner = total[:strip, :width]
    panel = jnp.concatenate([inner[:1] + carried[None], inner[1:]], 0).reshape(
        node_rows, group_cols
    )
    count = lax.axis_size("snap")
    group = lax.axis_index("snap")
    reach = count // 2

    def place(partial_value, moving, step):
        tile = contract(snapshots, moving)
        source = (group - step) % count * group_cols
        return lax.dynamic_update_slice(partial_value, tile, (jnp.int32(0), source))

    partial_value = place(jnp.zeros((group_cols, group_cols * count), jnp.float32), panel, 0)

    def turn(step, carry):
        moving, partial_value = carry
        moving = from_behind(moving, "snap", 1)
        return (moving, place(partial_value, moving, step))

    _, partial_value = lax.fori_loop(1, reach + 1, turn, (panel, partial_value))
    blocks = jnp.transpose(partial_value.reshape(group_cols, count, group_cols), (1, 2, 0))
    target = jnp.arange(count, dtype=jnp.int32)
    offset = (group - target) % count
    valid = (offset >= 1) & (offset <= count - 1 - reach)
    outgoing = jnp.where(valid[:, None, None], blocks, jnp.zeros((), jnp.float32))
    incoming = lax.all_to_all(outgoing, "snap", split_axis=0, concat_axis=0, tiled=True)
    partial_value = partial_value + jnp.transpose(incoming, (1, 0, 2)).reshape(
        group_cols, count * group_cols
    )
    summed = lax.psum_scatter(partial_value, "mesh", scatter_dimension=1, tiled=True)
    total_nodes = node_rows * lax.axis_size("mesh")
    return summed / math.sqrt(total_nodes)


ALL = ("h", "l", "x", "y", "c")
PLACE = ("l", "x")
TILE = ("y", "c")
GROUP = 128
STRIP = 128
SEAM = 16


def flat(h, l, x, y, c):
    return (((h * 2 + l) * 2 + x) * 2 + y) * 2 + c


def crossing(outer, flip):
    pairs = []
    for h in range(2):
        l = h if outer else 1 - h
        for x in range(2):
            for y in range(2):
                for c in range(2):
                    pairs.append((flat(h, l, x, y, c), flat(1 - h, h, x ^ flip, y, c)))
    return pairs


def middle_groups():
    four = [(x, y) for x in range(2) for y in range(2)]
    groups = [[flat(h, 1 - h, x, y, c) for h in range(2) for x, y in four] for c in range(2)]
    groups += [[flat(h, h, x, y, c) for x, y in four for c in range(2)] for h in range(2)]
    return groups


def owners(turn):
    pairs = []
    for h in range(2):
        for x in range(2):
            for y in range(2):
                for c in range(2):
                    lower = flat(0, h, x, 1, c)
                    upper = flat(1, c, y, 0, h)
                    down = (x + y + turn) % 2 == 0
                    pairs.append((flat(h, 1 - h, x, y, c), lower if down else upper))
    return pairs


MIDDLE_GROUPS = middle_groups()


def split(value):
    high = value.astype(jnp.bfloat16)
    return high, (value - high.astype(jnp.float32)).astype(jnp.bfloat16)


def product(left_high, left_low, right_high, right_low, turned=False):
    def one(a, b):
        return lax.dot_general(
            a, b, (((1 if turned else 0,), (0,)), ((), ())), preferred_element_type=jnp.float32
        )

    return one(left_high, right_high) + one(left_high, right_low) + one(left_low, right_high)


def own_kernel(
    rows,
    side_ref,
    seam_ref,
    ends_ref,
    field_ref,
    above_ref,
    below_ref,
    weight_ref,
    high_ref,
    low_ref,
    mine_ref,
    other_ref,
    sh,
    sl,
    ph,
    pw,
):
    wide = STRIP + 16
    line_number = lax.broadcasted_iota(jnp.int32, (SEAM, GROUP), 0)
    first_core = side_ref[0] == 0
    x, l = side_ref[2], side_ref[3]

    def line(main, left, right):
        return jnp.concatenate(
            [
                jnp.broadcast_to(left, (8, GROUP)),
                main,
                jnp.broadcast_to(right, (8, GROUP)),
            ],
            0,
        )

    def halo(ref, g):
        at = g * (STRIP + 8)
        end = at + STRIP
        return line(ref[at:end], ref[end : end + 1], ref[end + 1 : end + 2])

    body = rows * STRIP
    for g in range(4):
        columns = slice(g * GROUP, (g + 1) * GROUP)
        before = halo(above_ref, g)
        before_up = pltpu.roll(before, wide - 1, 0)
        carried = carried_next = None
        seam = jnp.zeros((SEAM, GROUP), jnp.float32)
        for r in range(-1, rows):
            n = r + 1
            if n < rows:
                if n in (0, rows - 1):
                    at = 0 if n == 0 else STRIP
                    main = ends_ref[g, at : at + STRIP]
                else:
                    main = field_ref[g, (n - 1) * STRIP : n * STRIP]
                sides = 2 * STRIP + n
                after = line(
                    main,
                    ends_ref[g, sides : sides + 1],
                    ends_ref[g, sides + 8 : sides + 9],
                )
                high, low = split(main)
                sh[n * STRIP : (n + 1) * STRIP, columns] = high
                sl[n * STRIP : (n + 1) * STRIP, columns] = low
            else:
                after = halo(below_ref, g)
            after_up = pltpu.roll(after, wide - 1, 0)
            weight = weight_ref[r] if r >= 0 else above_ref[4 * (STRIP + 8) :]
            top, top_up = 2.0 * before + after, 2.0 * before_up + after_up
            to_a, to_b = weight * (2.0 * top + top_up), weight * (top + 2.0 * top_up)
            if r >= 0:
                from_left = pltpu.roll(to_b + carried_next, 1, 0)
                total = to_a + carried + from_left
                beside = (
                    seam_ref[0] * from_left[8 + STRIP : 9 + STRIP] + seam_ref[1] * from_left[8:9]
                )
                seam = jnp.where(line_number == r, beside, seam)
                high, low = split(total[8 : 8 + STRIP])
                ph[r * STRIP : (r + 1) * STRIP, columns] = high
                pw[r * STRIP : (r + 1) * STRIP, columns] = low
            low_end, low_up = before + 2.0 * after, before_up + 2.0 * after_up
            carried = weight * (2.0 * low_end + low_up)
            carried_next = weight * (low_end + 2.0 * low_up)
            before, before_up = after, after_up
        high, low = split(seam)
        ph[body : body + SEAM, columns] = high
        pw[body : body + SEAM, columns] = low
    for a in range(2):
        left = slice(a * 256, (a + 1) * 256)
        tiles = [
            product(
                sh[:, left], sl[:, left], ph[:body, right], pw[:body, right]
            )
            for right in (slice(0, 256), slice(256, 512))
        ]
        mine = jnp.where(first_core, tiles[0], tiles[1])
        other = jnp.where(first_core, tiles[1], tiles[0])
        for i in range(2):
            rows_of = slice(i * GROUP, (i + 1) * GROUP)
            mine_ref[l ^ a, x ^ i] = mine[rows_of]
            other_ref[l ^ a, x ^ i] = other[rows_of]
    for turned_ref, panel in ((high_ref, ph), (low_ref, pw)):
        turned_ref[...] = panel[...].T


def early_kernel(high_ref, low_ref, s0, s1, s2, pair_ref, third_ref):
    h0, l0 = split(s0[...])
    h1, l1 = split(s1[...])
    sh = jnp.concatenate([h0, h1], 1)
    sl = jnp.concatenate([l0, l1], 1)
    pair_ref[...] = product(high_ref[...], low_ref[...], sh, sl, turned=True)
    sh, sl = split(s2[...])
    third_ref[...] = product(high_ref[...], low_ref[...], sh, sl, turned=True)


def cross_kernel(side_ref, high_ref, low_ref, last, pair_ref, third_ref, mine_ref, other_ref, fourth):
    core, half, x = side_ref[0], side_ref[1], side_ref[2]
    sh, sl = split(last[...])
    fourth[...] = product(high_ref[...], low_ref[...], sh, sl, turned=True)

    def place(h, c):
        for pair in range(2):
            for a in range(2):
                ref = mine_ref if (a if h else pair) == c else other_ref
                for i in range(2):
                    for j in range(2):
                        rows_of = slice((2 * a + i) * GROUP, (2 * a + i + 1) * GROUP)
                        if pair == 0:
                            block = pair_ref[rows_of, j * GROUP : (j + 1) * GROUP]
                        else:
                            block = (third_ref if j else fourth)[rows_of]
                        if h:
                            ref[(2 * (1 - pair) + (x ^ j)) * 2 + i] = block.T
                        else:
                            ref[(2 * a + i) * 2 + (x ^ j)] = block

    for h in range(2):
        for c in range(2):
            pl.when((half == h) & (core == c))(lambda: place(h, c))


VMEM = pl.BlockSpec(memory_space=pltpu.VMEM)
SMEM = pl.BlockSpec(memory_space=pltpu.SMEM)


def local_strips(snapshots, region_ids, conductivity):
    rows, width = region_ids.shape
    nodes = rows * STRIP
    field = snapshots.reshape(rows, width, GROUP)
    h, l, x, y, c = (lax.axis_index(a) for a in ALL)

    seam = jnp.concatenate(
        [field[:, 2 * STRIP], jnp.zeros((SEAM - rows, GROUP), jnp.float32)], 0
    )

    def strip_at(t):
        main = lax.dynamic_slice_in_dim(field, t * STRIP, STRIP, 1)
        return [jnp.concatenate([main.reshape(nodes, GROUP), seam], 0)]

    halves = [strip_at(2 * (1 - h) + (x ^ flip))[0] for flip in range(2)]
    near = [lax.ppermute(halves[0], ALL, crossing(False, 0))]

    parts = field.reshape(rows, 4, STRIP, GROUP)
    left = jnp.pad(parts[:, :3, STRIP - 1], ((0, 8 - rows), (1, 0), (0, 0)))
    right = jnp.pad(parts[:, 1:, 0], ((0, 8 - rows), (0, 1), (0, 0)))
    ends = jnp.concatenate(
        [parts[0], parts[rows - 1], jnp.transpose(left, (1, 0, 2)), jnp.transpose(right, (1, 0, 2))], 1
    )
    ends = jnp.concatenate([ends[2:], ends[:2]], 0)
    between = jnp.transpose(parts[1 : rows - 1], (1, 0, 2, 3)).reshape(4, -1, GROUP)
    between = jnp.concatenate([between[2:], between[:2]], 0)
    ends = lax.all_to_all(ends, PLACE, 0, 0, tiled=True)
    between = lax.all_to_all(between, PLACE, 0, 0, tiled=True)
    half, ends = lax.optimization_barrier((halves[1], ends))
    near.append(lax.ppermute(half, ALL, crossing(False, 1)))

    total_nodes = snapshots.shape[0] * 4
    weight = weights_of(region_ids, conductivity) / math.sqrt(total_nodes)
    weight = jnp.pad(weight, ((0, 0), (8, 8)))
    weight = lax.dynamic_slice_in_dim(weight, (2 * (1 - l) + x) * STRIP, STRIP + 16, 1)
    weight = jnp.broadcast_to(weight[:, :, None], (rows, STRIP + 16, GROUP))

    def edge(at, r):
        return jnp.concatenate(
            [
                ends[:, at : at + STRIP],
                ends[:, 2 * STRIP + r : 2 * STRIP + r + 1],
                ends[:, 2 * STRIP + 8 + r : 2 * STRIP + 9 + r],
                jnp.zeros((4, 6, GROUP), jnp.float32),
            ],
            1,
        ).reshape(4 * (STRIP + 8), GROUP)

    above = jnp.concatenate([edge(STRIP, rows - 1), weight[rows - 1]], 0)
    below = edge(0, 0)
    above = lax.ppermute(above, TILE, [(m, m + 1) for m in range(3)])
    below = lax.ppermute(below, TILE, [(m + 1, m) for m in range(3)])
    half, near[0], below = lax.optimization_barrier((halves[1], near[0], below))
    far = [lax.ppermute(half, ALL, crossing(True, 1))]
    half, near[1], above, below = lax.optimization_barrier((halves[0], near[1], above, below))
    far.append(lax.ppermute(half, ALL, crossing(True, 0)))

    side = jnp.stack([c, h, x, l]).astype(jnp.int32)
    seam_side = jnp.stack([(h == 0) & (x == 1), (h == 1) & (x == 0)]).astype(jnp.float32)
    seam_side = seam_side * jnp.array([1.0, -1.0], jnp.float32)
    blocks = jax.ShapeDtypeStruct((8, GROUP, GROUP), jnp.float32)
    own_blocks = jax.ShapeDtypeStruct((2, 2, GROUP, 2 * GROUP), jnp.float32)
    half_float = jax.ShapeDtypeStruct((4 * GROUP, nodes + SEAM), jnp.bfloat16)
    high, low, own_mine, own_other = pl.pallas_call(
        lambda *refs: own_kernel(rows, *refs),
        out_shape=(half_float, half_float, own_blocks, own_blocks),
        in_specs=[SMEM] * 2 + [VMEM] * 5,
        out_specs=(VMEM,) * 4,
        scratch_shapes=[pltpu.VMEM((nodes, 4 * GROUP), jnp.bfloat16)] * 2
        + [pltpu.VMEM((nodes + SEAM, 4 * GROUP), jnp.bfloat16)] * 2,
        compiler_params=pltpu.CompilerParams(vmem_limit_bytes=40 * 1024 * 1024),
        cost_estimate=pl.CostEstimate(flops=1, bytes_accessed=1, transcendentals=0),
    )(side, seam_side, ends, between, above, below, weight)

    def both_cores(mine, other):
        return mine + lax.ppermute(other, "c", [(0, 1), (1, 0)])

    own = both_cores(own_mine, own_other)
    wide = [jax.ShapeDtypeStruct((4 * GROUP, n * GROUP), jnp.float32) for n in (2, 1)]
    early = pl.pallas_call(
        early_kernel,
        out_shape=wide,
        in_specs=[VMEM] * 5,
        out_specs=[VMEM] * 2,
        compiler_params=pltpu.CompilerParams(vmem_limit_bytes=40 * 1024 * 1024),
        cost_estimate=pl.CostEstimate(flops=1, bytes_accessed=1, transcendentals=0),
    )(high, low, *near, far[0])
    cross_mine, cross_other = pl.pallas_call(
        cross_kernel,
        out_shape=(blocks, blocks),
        in_specs=[SMEM] + [VMEM] * 5,
        out_specs=(VMEM,) * 2,
        scratch_shapes=[pltpu.VMEM((4 * GROUP, GROUP), jnp.float32)],
        compiler_params=pltpu.CompilerParams(vmem_limit_bytes=40 * 1024 * 1024),
        cost_estimate=pl.CostEstimate(flops=1, bytes_accessed=1, transcendentals=0),
    )(side, high, low, far[1], *early)

    cross = both_cores(cross_mine, cross_other)
    own = own[0] + lax.ppermute(own[1], "l", [(0, 1), (1, 0)])
    own = own[0] + lax.ppermute(own[1], "x", [(0, 1), (1, 0)])
    to_holder = [
        (flat(i, j, k, 1 - i, n), flat(i, j, k, i, n))
        for i in range(2)
        for j in range(2)
        for k in range(2)
        for n in range(2)
    ]
    own = own + lax.ppermute(own, ALL, to_holder)

    cross = lax.all_to_all(cross, ALL, 0, 0, tiled=True, axis_index_groups=MIDDLE_GROUPS)
    cross = jnp.sum(cross, 0)
    even = (x + y) % 2 == 0
    turned = cross.T
    cross_pair = [
        lax.ppermute(jnp.where(even, cross, turned), ALL, owners(0)),
        lax.ppermute(jnp.where(even, turned, cross), ALL, owners(1)),
    ]
    swapped = (x + h) % 2 == 1
    left = jnp.where(swapped, cross_pair[1], cross_pair[0])
    right = jnp.where(swapped, cross_pair[0], cross_pair[1])
    return jnp.where(y == h, own, jnp.concatenate([left, right], 1))


def solution(mesh):
    sizes = (mesh.shape["snap"], mesh.shape["mesh"])

    def whole(snapshots, region_ids, conductivity):
        width = region_ids.shape[1]
        if sizes == (8, 4) and snapshots.shape[1] == 8 * GROUP and width == 4 * STRIP:
            parts = Mesh(mesh.devices.reshape(2, 2, 2, 2, 2), ALL)
            return jax.shard_map(
                local_strips,
                mesh=parts,
                in_specs=(P(TILE, ("h", "l", "x")), P(TILE, None), P()),
                out_specs=P(("h", "l", "x"), TILE),
                check_vma=False,
            )(snapshots, region_ids, conductivity)
        return jax.shard_map(
            local_ring,
            mesh=mesh,
            in_specs=(P("mesh", "snap"), P("mesh", None), P()),
            out_specs=P("snap", "mesh"),
            check_vma=False,
        )(snapshots, region_ids, conductivity)

    return whole
```
